128 devices in a mesh: dp: 16 (over x, z), fsdp: 8 (over y, core).
Axes of the slice: x: 4, y: 4, z: 4, core: 2. Of those that a mesh axis runs over, the one named last changes fastest.
Arguments:
- grad_shards: bfloat16 [16, 8192, 6144], P('dp', None, 'fsdp'), may hold values from -36 to 36
- hadamard_signs: int32 [6144], P('fsdp'), may hold values from 0 to 1
- scale_index: int32 [24, 8192], P('fsdp'), may hold values from 0 to 15
- scale_table: float32 [16], replicated, may hold values from 0.004 to 0.2
- master: float32 [8192, 6144], P('dp', 'fsdp'), may hold values from -6 to 6
- mean_moment: float32 [8192, 6144], P('dp', 'fsdp'), may hold values from -3 to 3
- var_moment: float32 [8192, 6144], P('dp', 'fsdp'), may hold values from 0.01 to 1
Outputs:
- new_master: float32 [8192, 6144], P('dp', 'fsdp')
- new_mean: float32 [8192, 6144], P('dp', 'fsdp')
- new_var: float32 [8192, 6144], P('dp', 'fsdp')
- weights: bfloat16 [8192, 6144], P('dp')
The draws below stay inside these ranges and needn't reach their ends.
All inputs are finite; a program needn't handle non-finite values.
Results may differ from the reference program's by a relative error of at most 0.0019.
Values may be sent and summed in bfloat16 or wider, within the bound.
No kernel may reach another device: no remote copies, remote signals or barrier semaphores. Data moves between devices by JAX's collectives and lax.ppermute only.
A program may use at most 192 MiB of HBM per device.

```python
import math
import jax
import jax.numpy as jnp
from jax import lax

D = 6144
ROWS = 8192
TILE = 256
LEVELS = 16
TILES = 24
N_DP = 16


def draw_grad_shards(key, part):
    key = jax.random.fold_in(key, 11)
    key_own = jax.random.fold_in(key, 0)
    key_common = jax.random.fold_in(key, 1)
    key_lower = jax.random.fold_in(key, 3)
    key_upper = jax.random.fold_in(key, 4)
    half_count = N_DP // 2
    few_count = half_count // 4
    lower_order = jax.random.permutation(key_lower, half_count)
    upper_order = jax.random.permutation(key_upper, N_DP - half_count)
    linked = jnp.concatenate([lower_order < few_count, upper_order >= few_count])
    linked_rows = jnp.repeat(linked, ROWS // N_DP)[None, :, None]
    row_pos = jnp.arange(ROWS, dtype=jnp.float32) / (ROWS - 1)
    row_factor = (2.0 * (1.0 + 2.0 * row_pos))[None, :, None]
    own = jax.random.truncated_normal(key_own, -6.0, 6.0, (N_DP, ROWS, D), jnp.float32)
    common = jax.random.truncated_normal(key_common, -6.0, 6.0, (1, ROWS, D), jnp.float32)
    own_weight = jnp.where(linked_rows, 0.3122, 1.0)
    common_weight = jnp.where(linked_rows, 0.95, 0.0)
    values = (own_weight * own + common_weight * common) * row_factor
    values = jnp.clip(values, -36.0, 36.0)
    return values.astype(jnp.bfloat16)


def touch_ends(result, own_key, smallest, high):
    index_at = [jax.random.randint(jax.random.fold_in(own_key, axis), (), 0, length) for axis, length in enumerate(result.shape)]
    longest = result.shape.index(max(result.shape))
    next_to = index_at[:longest] + [(index_at[longest] + 1) % result.shape[longest]] + index_at[longest + 1:]
    return result.at[tuple(index_at)].set(smallest).at[tuple(next_to)].set(high)


def block_scale(stream_key, shape, pieces, least, high):
    factor_of = 1.0
    for dim, parts in pieces:
        draws = jax.random.uniform(jax.random.fold_in(jax.random.fold_in(stream_key, 6), dim), (parts,), jnp.float32, least / len(pieces), high / len(pieces))
        factor_of = factor_of * jnp.repeat(jnp.exp(draws), shape[dim] // parts).reshape((-1,) + (1,) * (len(shape) - 1 - dim))
    return factor_of


def centred(rng, shape, scale, bound, shards=(), kind=jnp.bfloat16):
    level = block_scale(rng, shape, shards, -0.22, 0.18) if shards else 1.0
    entries = jax.random.normal(rng, shape, jnp.float32) * scale * level
    return jnp.minimum(jnp.maximum(entries, -bound), bound).astype(kind)


def setup_inputs(seed: int = 0) -> dict:
    keys = jax.random.split(jax.random.key(seed), 8)
    return {
        "grad_shards": draw_grad_shards(jax.random.fold_in(keys[7], 71), 0),
        "hadamard_signs": touch_ends(jax.random.randint(keys[1], (D,), 0, 2), jax.random.fold_in(keys[1], 1), 0, 1).astype(jnp.int32),
        "scale_index": touch_ends(jax.random.randint(keys[2], (TILES, ROWS), 0, LEVELS), jax.random.fold_in(keys[2], 1), 0, LEVELS - 1).astype(jnp.int32),
        "scale_table": jnp.clip(jnp.exp(jax.random.uniform(keys[3], (LEVELS,), jnp.float32, math.log(0.004), math.log(0.2))), 0.004, 0.2),
        "master": centred(keys[4], (ROWS, D), 1.0, 6.0, ((0, 16), (1, 8)), jnp.float32),
        "mean_moment": centred(keys[5], (ROWS, D), 0.3, 3.0, ((0, 16), (1, 8)), jnp.float32),
        "var_moment": jnp.clip(jnp.exp(math.log(1.0) - 4.6051702 * jax.random.uniform(keys[6], (ROWS, D), jnp.float32) ** block_scale(keys[6], (ROWS, D), ((0, 16), (1, 8)), -0.2, 0.2)), 0.01, 1.0),
    }


def hadamard(length, dtype):
    row_index = lax.broadcasted_iota(jnp.int32, (length, length), 0)
    col_index = lax.broadcasted_iota(jnp.int32, (length, length), 1)
    common_bits = row_index & col_index
    parity = jnp.zeros((length, length), jnp.int32)
    for bit_pos in range(length.bit_length() - 1):
        parity = parity ^ common_bits >> bit_pos & 1
    return (1 - 2 * parity).astype(dtype)

def lookup(table, index):
    levels = jnp.arange(table.shape[0], dtype=jnp.int32)
    hits = index[..., None] == levels
    return lax.optimization_barrier(jnp.sum(jnp.where(hits, table, jnp.zeros_like(table)), axis=-1))

def encode(grad_rows, sign_low, scales, hmat_low):
    count, width = grad_rows.shape
    length = hmat_low.shape[0]
    tiles = width // length
    signed = grad_rows * sign_low
    rotated = jnp.dot(signed.reshape(count * tiles, length), hmat_low, preferred_element_type=jnp.float32)
    rotated = rotated.reshape(count, tiles, length) * (1.0 / math.sqrt(length))
    coded = jnp.clip(rotated / scales[:, :, None], -127.0, 127.0)
    return coded.astype(jnp.bfloat16)

def reference(grad_shards, hadamard_signs, scale_index, scale_table, master, mean_moment, var_moment):
    hmat_low = hadamard(TILE, jnp.bfloat16)
    hmat_high = hadamard(TILE, jnp.float32)
    sign_low = (2 * hadamard_signs - 1).astype(jnp.bfloat16)
    sign_high = (2 * hadamard_signs - 1).astype(jnp.float32)
    all_scales = jnp.transpose(lookup(scale_table, scale_index))

    def add_replica(carry, replica):
        coded = encode(replica, sign_low, all_scales, hmat_low)
        return (carry + coded.astype(jnp.float32), None)
    start = jnp.zeros((ROWS, D // TILE, TILE), jnp.float32)
    summed, _ = lax.scan(add_replica, start, grad_shards)
    dequant = summed * all_scales[:, :, None]
    plain = jnp.dot(dequant.reshape(-1, TILE), hmat_high, precision=lax.Precision.HIGHEST, preferred_element_type=jnp.float32)
    plain = (plain * (1.0 / math.sqrt(TILE))).reshape(ROWS, D) * sign_high
    squares = jnp.sum(plain * plain)
    limit = 4.0 * math.sqrt(ROWS * D)
    grad = plain * (limit / jnp.maximum(jnp.sqrt(squares), limit))
    new_mean = 0.9 * mean_moment + 0.1 * grad
    new_var = 0.95 * var_moment + 0.05 * grad * grad
    update = new_mean / (1.0 - 0.9 ** 10) / (jnp.sqrt(new_var / (1.0 - 0.95 ** 10)) + 1e-08)
    new_master = master - 0.02 * (update + 0.1 * master)
    return (new_master, new_mean, new_var, new_master.astype(jnp.bfloat16))
```

```python
import functools
import math

import jax
import jax.numpy as jnp
from jax import lax
from jax.experimental import pallas as pl
from jax.experimental.pallas import tpu as pltpu
from jax.sharding import PartitionSpec as P

D = 6144
ROWS = 8192
TILE = 256
WIDTH = 768
TILES = WIDTH // TILE
SIDE = 4
BLOCK = 256
RING0, RING1 = (2, 1), (3, 0)
LIMIT = 4.0 * math.sqrt(ROWS * D)
VMEM_BYTES = 32 * 1024 * 1024


def hadamard(length):
    row_index = lax.broadcasted_iota(jnp.int32, (length, length), 0)
    col_index = lax.broadcasted_iota(jnp.int32, (length, length), 1)
    common_bits = row_index & col_index
    parity = jnp.zeros((length, length), jnp.int32)
    for bit_pos in range(length.bit_length() - 1):
        parity = parity ^ common_bits >> bit_pos & 1
    return 1 - 2 * parity


def hop(value, axis, step):
    if axis == "x":
        pairs = [(i, (i // 4 + step) % 4 * 4 + i % 4) for i in range(16)]
    elif axis == "z":
        pairs = [(i, i // 4 * 4 + (i % 4 + step) % 4) for i in range(16)]
    elif axis == "y":
        pairs = [(i, (i // 2 + step) % 4 * 2 + i % 2) for i in range(8)]
    else:
        pairs = [(i, i ^ 1) for i in range(8)]
    return lax.ppermute(value, "dp" if axis in "xz" else "fsdp", pairs)


def row_scales(index_ref, table_ref):
    index = index_ref[...]
    scale = jnp.zeros(index.shape, jnp.float32)
    for level in range(table_ref.shape[0]):
        scale = jnp.where(index == level, table_ref[level], scale)
    ones = jnp.ones((8 - index.shape[0], index.shape[1]), jnp.float32)
    return jnp.concatenate([scale, ones], axis=0).T


def encode_kernel(count, place_ref, table_ref, grad_ref, index_ref, hmat_ref, *refs):
    arrived, out_ref = refs[:count], refs[count]
    steps = 1.0 / (math.sqrt(TILE) * row_scales(index_ref, table_ref))
    for tile in range(TILES):
        cols = slice(tile * TILE, (tile + 1) * TILE)
        rotated = jnp.dot(grad_ref[:, cols], hmat_ref[cols, :], preferred_element_type=jnp.float32)
        code = jnp.clip(rotated * steps[:, tile : tile + 1], -127.0, 127.0).astype(jnp.bfloat16)
        if count:
            total = code.astype(jnp.float32)
            for ref in arrived:
                total = total + ref[:, cols].astype(jnp.float32)
            code = total.astype(out_ref.dtype)
        out_ref[:, cols] = code


def encode(place, table, grad, index, hmat, half, near, ring, arrived=(), dtype=jnp.bfloat16):
    count = len(ring)

    def block(j, place_ref):
        far = ring[0] + j * (ring[1] - ring[0])
        first, second = place_ref[half], place_ref[1 - half]
        first, second = (first + near) % SIDE, (second + far) % SIDE
        x, z = (first, second) if half == 0 else (second, first)
        return (x * SIDE + z) * 2 + half

    whole = pl.BlockSpec((BLOCK, WIDTH), lambda j, place_ref: (j, 0))
    return pl.pallas_call(
        functools.partial(encode_kernel, len(arrived)),
        out_shape=jax.ShapeDtypeStruct((count * BLOCK, WIDTH), dtype),
        grid_spec=pltpu.PrefetchScalarGridSpec(
            num_scalar_prefetch=1,
            grid=(count,),
            in_specs=[
                pl.BlockSpec(memory_space=pltpu.SMEM),
                pl.BlockSpec((BLOCK, WIDTH), lambda j, place_ref: (block(j, place_ref), 0)),
                pl.BlockSpec((TILES, BLOCK), lambda j, place_ref: (0, block(j, place_ref))),
                pl.BlockSpec((WIDTH, TILE), lambda j, place_ref: (0, 0)),
            ]
            + [whole] * len(arrived),
            out_specs=whole,
        ),
        compiler_params=pltpu.CompilerParams(vmem_limit_bytes=VMEM_BYTES),
        cost_estimate=pl.CostEstimate(
            flops=2 * count * BLOCK * WIDTH * TILE,
            bytes_accessed=count * BLOCK * WIDTH * 2 * (2 + len(arrived)),
            transcendentals=0,
        ),
    )(place, table, grad, index, hmat, *arrived)


def first_axis(place, table, grad, index, hmat, half):
    axis = "xz"[half]
    code = functools.partial(encode, place, table, grad, index, hmat, half)
    up_far = hop(code(2, RING0), axis, 1)
    down_far = hop(code(2, RING1), axis, -1)
    up_own = hop(code(1, RING1), axis, 1)
    down_own = hop(code(-1, RING0), axis, -1)
    up_sum = hop(code(1, RING0, (up_far,)), axis, 1)
    down_sum = hop(code(-1, RING1, (down_far,)), axis, -1)
    sum0 = code(0, RING0, (up_sum, down_own), jnp.float32)
    sum1 = code(0, RING1, (up_own, down_sum), jnp.float32)
    by_offset = {}
    for ring, total in ((RING0, sum0), (RING1, sum1)):
        for j, far in enumerate(ring):
            by_offset[far] = total[j * BLOCK : (j + 1) * BLOCK]
    return by_offset


def second_axis(blocks, half):
    axis = "zx"[half]
    low, mid = slice(0, BLOCK // 2), slice(BLOCK // 2, BLOCK)
    send = lambda v, step: hop(v.astype(jnp.bfloat16), axis, step)
    up_far = send(blocks[2][low], 1)
    down_far = send(blocks[2][mid], -1)
    up_own = send(blocks[1][mid], 1)
    down_own = send(blocks[3][low], -1)
    up_sum = send(blocks[1][low] + up_far.astype(jnp.float32), 1)
    down_sum = send(blocks[3][mid] + down_far.astype(jnp.float32), -1)
    return blocks[0], (up_sum, down_own), (up_own, down_sum)


def decode_kernel(place_ref, table_ref, own_ref, up0_ref, down0_ref, up1_ref, down1_ref, index_ref, hmat_ref, plain_ref, square_ref):
    half_rows = BLOCK // 2
    scales = row_scales(index_ref, table_ref)
    f32 = jnp.float32
    square = jnp.zeros((8, 128), f32)
    for part, (up_ref, down_ref) in enumerate(((up0_ref, down0_ref), (up1_ref, down1_ref))):
        rows = slice(part * half_rows, (part + 1) * half_rows)
        total = own_ref[rows, :] + up_ref[...].astype(f32) + down_ref[...].astype(f32)
        for tile in range(TILES):
            cols = slice(tile * TILE, (tile + 1) * TILE)
            value = total[:, cols] * scales[rows, tile : tile + 1]
            plain = jnp.zeros((half_rows, TILE), f32)
            for _ in range(3):
                piece = value.astype(jnp.bfloat16)
                plain = plain + jnp.dot(piece, hmat_ref[:, cols], preferred_element_type=f32)
                value = value - piece.astype(f32)
            plain = plain * (1.0 / math.sqrt(TILE))
            plain_ref[rows, cols] = plain
            square = square + jnp.sum((plain * plain).reshape(-1, 8, TILE), axis=0).reshape(8, 2, 128).sum(axis=1)
    square_ref[...] = square


def decode(place, table, terms, index, hmat_t, half):
    own, (up0, down0), (up1, down1) = terms
    block = lambda j, place_ref: (0, (place_ref[0] * SIDE + place_ref[1]) * 2 + half)
    full = pl.BlockSpec((BLOCK, WIDTH), lambda j, place_ref: (0, 0))
    part = pl.BlockSpec((BLOCK // 2, WIDTH), lambda j, place_ref: (0, 0))
    return pl.pallas_call(
        decode_kernel,
        out_shape=(
            jax.ShapeDtypeStruct((BLOCK, WIDTH), jnp.float32),
            jax.ShapeDtypeStruct((8, 128), jnp.float32),
        ),
        grid_spec=pltpu.PrefetchScalarGridSpec(
            num_scalar_prefetch=1,
            grid=(1,),
            in_specs=[
                pl.BlockSpec(memory_space=pltpu.SMEM),
                full,
                part,
                part,
                part,
                part,
                pl.BlockSpec((TILES, BLOCK), block),
                pl.BlockSpec((TILE, WIDTH), lambda j, place_ref: (0, 0)),
            ],
            out_specs=(full, pl.BlockSpec((8, 128), lambda j, place_ref: (0, 0))),
        ),
        compiler_params=pltpu.CompilerParams(vmem_limit_bytes=VMEM_BYTES),
    )(place, table, own, up0, down0, up1, down1, index, hmat_t)


def total_squares(square):
    for axis in "xzy":
        square = square + hop(square, axis, 1) + (hop(square, axis, 2) + hop(square, axis, 3))
    return square + hop(square, "core", 1)


def updated(plain, square, master, mean, var):
    factor = LIMIT / jnp.maximum(jnp.sqrt(jnp.sum(square)), LIMIT)
    grad = plain * factor
    new_mean = 0.9 * mean + 0.1 * grad
    new_var = 0.95 * var + 0.05 * grad * grad
    update = new_mean / (1.0 - 0.9**10) / (jnp.sqrt(new_var / (1.0 - 0.95**10)) + 1e-08)
    return master - 0.02 * (update + 0.1 * master), new_mean, new_var


def weights_kernel(square_ref, plain0_ref, plain1_ref, master_ref, mean_ref, var_ref, out_ref):
    for half, plain_ref in enumerate((plain0_ref, plain1_ref)):
        rows = slice(half * BLOCK, (half + 1) * BLOCK)
        new_master, _, _ = updated(plain_ref[...], square_ref[...], master_ref[rows, :], mean_ref[rows, :], var_ref[rows, :])
        out_ref[rows, :] = new_master.astype(jnp.bfloat16)


def state_kernel(square_ref, plain0_ref, plain1_ref, master_ref, mean_ref, var_ref, *out_refs):
    for half, plain_ref in enumerate((plain0_ref, plain1_ref)):
        rows = slice(half * BLOCK, (half + 1) * BLOCK)
        values = updated(plain_ref[...], square_ref[...], master_ref[rows, :], mean_ref[rows, :], var_ref[rows, :])
        for ref, value in zip(out_refs, values, strict=True):
            ref[rows, :] = value


def adamw(kernel, out_shape, square, plains, master, mean, var):
    step = WIDTH // 6
    half = pl.BlockSpec((BLOCK, step), lambda j: (0, j))
    full = pl.BlockSpec((2 * BLOCK, step), lambda j: (0, j))
    return pl.pallas_call(
        kernel,
        out_shape=out_shape,
        grid=(6,),
        in_specs=[pl.BlockSpec((8, 128), lambda j: (0, 0)), half, half, full, full, full],
        out_specs=jax.tree.map(lambda _: full, out_shape),
        compiler_params=pltpu.CompilerParams(vmem_limit_bytes=VMEM_BYTES),
        cost_estimate=pl.CostEstimate(flops=20 * 512 * 768, bytes_accessed=10 * 512 * 768 * 4, transcendentals=512 * 768),
    )(square, *plains, master, mean, var)


def gather_columns(low):
    fsdp = lax.axis_index("fsdp")
    chip, core = fsdp // 2, fsdp % 2
    moved = [low, hop(low, "y", 1), hop(low, "y", -1), hop(low, "y", 2)]
    other = [hop(v, "core", 1) for v in moved]
    out = jnp.zeros((low.shape[0], D), low.dtype)
    for mine, theirs, step in zip(moved, other, (0, 1, -1, 2), strict=True):
        source = (chip - step) % SIDE * 2
        out = lax.dynamic_update_slice(out, mine, (0, (source + core) * WIDTH))
        out = lax.dynamic_update_slice(out, theirs, (0, (source + 1 - core) * WIDTH))
    return out


def on_device(grad_shards, hadamard_signs, scale_index, scale_table, master, mean_moment, var_moment):
    grad = grad_shards[0]
    dp = lax.axis_index("dp")
    place = jnp.stack([dp // SIDE, dp % SIDE]).astype(jnp.int32)
    sign = 2 * hadamard_signs - 1
    hmat = hadamard(TILE)
    hmat_in = (jnp.tile(hmat, (TILES, 1)) * sign[:, None]).astype(jnp.bfloat16)
    hmat_out = (jnp.tile(hmat, (1, TILES)) * sign[None, :]).astype(jnp.bfloat16)
    plains, squares = [], []
    firsts = [first_axis(place, scale_table, grad, scale_index, hmat_in, half) for half in (0, 1)]
    for half in (0, 1):
        terms = second_axis(firsts[half], half)
        plain, square = decode(place, scale_table, terms, scale_index, hmat_out, half)
        plains.append(plain)
        squares.append(square)
    square = total_squares(squares[0] + squares[1])
    state = jax.ShapeDtypeStruct((2 * BLOCK, WIDTH), jnp.float32)
    low = adamw(weights_kernel, jax.ShapeDtypeStruct((2 * BLOCK, WIDTH), jnp.bfloat16), square, plains, master, mean_moment, var_moment)
    new_master, new_mean, new_var = adamw(state_kernel, (state,) * 3, square, plains, master, mean_moment, var_moment)
    return new_master, new_mean, new_var, gather_columns(low)


def solution(mesh):
    return jax.shard_map(
        on_device,
        mesh=mesh,
        in_specs=(
            P("dp", None, "fsdp"),
            P("fsdp"),
            P("fsdp", None),
            P(),
            P("dp", "fsdp"),
            P("dp", "fsdp"),
            P("dp", "fsdp"),
        ),
        out_specs=(P("dp", "fsdp"), P("dp", "fsdp"), P("dp", "fsdp"), P("dp", None)),
        check_vma=False,
    )
```

```python
import functools
import math

import jax
import jax.numpy as jnp
import ml_dtypes
import numpy as np
from jax import lax
from jax.experimental import pallas as pl
from jax.experimental.pallas import tpu as pltpu
from jax.sharding import PartitionSpec as P

D = 6144
ROWS = 8192
TILE = 256
WIDTH = 768
TILES = WIDTH // TILE
SIDE = 4
BLOCK = 512
PART = 256
STEP = 128
RING0, RING1 = (2, 1), (3, 0)
LIMIT = 4.0 * math.sqrt(ROWS * D)
VMEM_BYTES = 24 * 1024 * 1024


def hadamard(length):
    index = np.arange(length)
    common_bits = index[:, None] & index[None, :]
    parity = np.zeros((length, length), np.int32)
    for bit_pos in range(length.bit_length() - 1):
        parity = parity ^ common_bits >> bit_pos & 1
    return (1 - 2 * parity).astype(ml_dtypes.bfloat16)


def hop(value, axis, step):
    pairs = []
    for device in range(128):
        x, z, core = device // 32, device // 8 % SIDE, device % 2
        if (axis == "first") == (core == 0):
            x = (x + step) % SIDE
        else:
            z = (z + step) % SIDE
        pairs.append((device, (x * SIDE + z) * 8 + device % 8))
    return lax.ppermute(value, ("dp", "fsdp"), pairs)


def in_hbm(value):
    return pltpu.with_memory_space_constraint(value, pltpu.HBM)


def row_scales(index_refs, table_ref, inverse):
    index = jnp.concatenate([ref[...] for ref in index_refs], axis=1)
    scale = jnp.zeros(index.shape, jnp.float32)
    for level in range(table_ref.shape[0]):
        scale = jnp.where(index == level, table_ref[level], scale)
    if inverse:
        scale = 1.0 / (math.sqrt(TILE) * scale)
    ones = jnp.ones((8 - index.shape[0], index.shape[1]), jnp.float32)
    return jnp.concatenate([scale, ones], axis=0).T


def encode_kernel(counts, place_ref, table_ref, sign_ref, hmat_ref, *refs):
    jobs = len(counts)
    inputs, out_refs = iter(refs[:-jobs]), refs[-jobs:]
    grad_refs, index_refs, arrived_refs = [], [], []
    for count in counts:
        grad_refs.append(next(inputs))
        index_refs.append(next(inputs))
        arrived_refs.append([next(inputs) for _ in range(count)])
    steps = row_scales(index_refs, table_ref, True)
    sign = (2 * sign_ref[...] - 1).astype(jnp.bfloat16)
    for tile in range(TILES):
        cols = slice(tile * TILE, (tile + 1) * TILE)
        signed = jnp.concatenate([ref[:, cols] for ref in grad_refs], axis=0) * sign[:, cols]
        rotated = jnp.dot(signed, hmat_ref[...], preferred_element_type=jnp.float32)
        codes = jnp.clip(rotated * steps[:, tile : tile + 1], -127.0, 127.0).astype(jnp.bfloat16)
        for job in range(jobs):
            code = codes[job * PART : (job + 1) * PART]
            if arrived_refs[job]:
                total = code.astype(jnp.float32)
                for ref in arrived_refs[job]:
                    total = total + ref[:, cols].astype(jnp.float32)
                code = total.astype(out_refs[job].dtype)
            out_refs[job][:, cols] = code


def block_at(place_ref, near, far):
    place = place_ref[0]
    x, z, core = place // (2 * SIDE), place // 2 % SIDE, place % 2
    x, z = x + jnp.where(core == 0, near, far), z + jnp.where(core == 0, far, near)
    return lax.rem(x, SIDE) * SIDE + lax.rem(z, SIDE)


def encode(place, table, sign, grad, index, hmat, grid, jobs):
    in_specs = [
        pl.BlockSpec(memory_space=pltpu.SMEM),
        pl.BlockSpec((1, WIDTH), lambda *_: (0, 0)),
        pl.BlockSpec((TILE, TILE), lambda *_: (0, 0)),
    ]
    operands, out_specs, out_shape = [table, sign, hmat], [], []
    parts = BLOCK // PART
    for near, far, arrived, spec, shape, dtype in jobs:
        rows = functools.partial(lambda near, far, i, j, place_ref: block_at(place_ref, near, far(i)) * parts + j, near, far)
        in_specs.append(pl.BlockSpec((PART, WIDTH), functools.partial(lambda rows, *at: (rows(*at), 0), rows)))
        in_specs.append(pl.BlockSpec((TILES, PART), functools.partial(lambda rows, *at: (0, rows(*at)), rows)))
        operands += [grad, index]
        for value, its_spec in arrived:
            in_specs.append(its_spec)
            operands.append(value)
        out_specs.append(spec)
        out_shape.append(jax.ShapeDtypeStruct(shape, dtype))
    blocks = len(jobs) * grid[0] * parts
    return pl.pallas_call(
        functools.partial(encode_kernel, [len(job[2]) for job in jobs]),
        out_shape=out_shape,
        grid_spec=pltpu.PrefetchScalarGridSpec(num_scalar_prefetch=1, grid=grid, in_specs=in_specs, out_specs=out_specs),
        compiler_params=pltpu.CompilerParams(vmem_limit_bytes=VMEM_BYTES),
        cost_estimate=pl.CostEstimate(flops=2 * blocks * PART * WIDTH * TILE, bytes_accessed=blocks * PART * WIDTH * 6, transcendentals=0),
    )(place, *operands)


def paired(ring):
    return lambda i: ring[0] + i * (ring[1] - ring[0])


def reduce_scatter(place, table, sign, grad, index, hmat, beside):
    code = functools.partial(encode, place, table, sign, grad, index, hmat)
    pair = ((2, BLOCK, WIDTH), jnp.bfloat16)
    both = pl.BlockSpec((None, PART, WIDTH), lambda i, j, place_ref: (i, j, 0))
    grid = (2, BLOCK // PART)

    def round_of(*plan):
        jobs = [(near, paired(ring), [(v, both) for v in arrived], both, *pair) for _, near, ring, arrived in plan]
        codes = code(grid, jobs)
        return [hop(v, "first", step) for v, (step, *_) in zip(codes, plan, strict=True)], codes

    (up_far, down_far), far_codes = round_of((1, 2, RING0, ()), (-1, 2, RING1, ()))
    packed = lax.all_gather(beside(far_codes[0]), "fsdp")
    (up_own, down_own), _ = round_of((1, 1, RING1, ()), (-1, 3, RING0, ()))
    (up_sum, down_sum), _ = round_of((1, 1, RING0, (up_far,)), (-1, 3, RING1, (down_far,)))
    jobs = []
    single = pl.BlockSpec((PART, WIDTH), lambda i, j, place_ref: (j, 0))
    for ring, values in ((RING0, (up_sum, down_own)), (RING1, (up_own, down_sum))):
        for slot, offset in enumerate(ring):
            spec = pl.BlockSpec((None, PART, WIDTH), functools.partial(lambda slot, i, j, place_ref: (slot, j, 0), slot))
            dtype = jnp.bfloat16 if offset else jnp.float32
            far_of = functools.partial(lambda offset, i: offset, offset)
            jobs.append((0, far_of, [(v, spec) for v in values], single, (BLOCK, WIDTH), dtype))
    sums = dict(zip(RING0 + RING1, code((1, BLOCK // PART), jobs), strict=True))
    return [sums[0]] + [in_hbm(hop(sums[k], "second", k)) for k in (2, 1, 3)], packed


def decode_kernel(place_ref, table_ref, sign_ref, hmat_ref, own_ref, two_ref, one_ref, three_ref, index_ref, after_ref, plain_ref, low_ref, square_ref, sum_ref):
    del after_ref
    f32 = jnp.float32
    first = pl.program_id(0) == 0

    @pl.when(first)
    def _():
        sum_ref[...] = jnp.zeros_like(sum_ref)

    scales = row_scales([index_ref], table_ref, False) * (1.0 / math.sqrt(TILE))
    sign = (2 * sign_ref[...] - 1).astype(f32)
    square = sum_ref[...]
    for tile in range(TILES):
        cols = slice(tile * TILE, (tile + 1) * TILE)
        value = own_ref[:, cols] + two_ref[:, cols].astype(f32) + one_ref[:, cols].astype(f32) + three_ref[:, cols].astype(f32)
        plain = jnp.zeros(value.shape, f32)
        for _ in range(3):
            piece = value.astype(jnp.bfloat16)
            plain = plain + jnp.dot(piece, hmat_ref[...], preferred_element_type=f32)
            value = value - piece.astype(f32)
        plain = plain * scales[:, tile : tile + 1] * sign[:, cols]
        plain_ref[:, cols] = plain

        @pl.when(first)
        def _():
            low_ref[:, cols] = plain.astype(jnp.bfloat16)

        parts = jnp.sum((plain * plain).reshape(-1, 8, TILE), axis=0)
        square = square + parts[:, :128] + parts[:, 128:]
    sum_ref[...] = square
    square_ref[...] = jnp.broadcast_to(square, square_ref.shape)


def decode(place, table, sign, terms, index, hmat, packed, copies):
    parts = BLOCK // PART
    single = pl.BlockSpec((PART, WIDTH), lambda j, place_ref: (j, 0))
    return pl.pallas_call(
        decode_kernel,
        out_shape=(
            jax.ShapeDtypeStruct((BLOCK, WIDTH), jnp.float32),
            pltpu.HBM((PART, WIDTH), jnp.bfloat16),
            pltpu.HBM((copies, 8, 128), jnp.float32),
        ),
        grid_spec=pltpu.PrefetchScalarGridSpec(
            num_scalar_prefetch=1,
            grid=(parts,),
            in_specs=[
                pl.BlockSpec(memory_space=pltpu.SMEM),
                pl.BlockSpec((1, WIDTH), lambda j, place_ref: (0, 0)),
                pl.BlockSpec((TILE, TILE), lambda j, place_ref: (0, 0)),
                *[single] * 4,
                pl.BlockSpec((TILES, PART), lambda j, place_ref: (0, block_at(place_ref, 0, 0) * parts + j)),
                pl.BlockSpec((1, 1, 16, 128), lambda j, place_ref: (0, 0, 0, 0)),
            ],
            out_specs=(
                single,
                pl.BlockSpec((PART, WIDTH), lambda j, place_ref: (0, 0)),
                pl.BlockSpec((copies, 8, 128), lambda j, place_ref: (0, 0, 0)),
            ),
            scratch_shapes=[pltpu.VMEM((8, 128), jnp.float32)],
        ),
        compiler_params=pltpu.CompilerParams(vmem_limit_bytes=VMEM_BYTES),
        cost_estimate=pl.CostEstimate(flops=6 * 512 * WIDTH * TILE, bytes_accessed=512 * WIDTH * 14, transcendentals=0),
    )(place, table, sign, hmat, *terms, index, packed)


def total_squares(square):
    square = jnp.sum(lax.all_to_all(square, "fsdp", 0, 0), axis=0)
    copies = jnp.broadcast_to(square, (lax.axis_size("dp"), *square.shape))
    return lax.all_to_all(copies, "dp", 0, 0)


MEAN_SCALE = 0.02 / (1.0 - 0.9**10)
VAR_SCALE = 1.0 / (1.0 - 0.95**10)


def clip_factor(square_ref):
    square = jnp.sum(square_ref[...], axis=0)
    square = jnp.sum(jnp.sum(square, axis=0, keepdims=True), axis=1, keepdims=True)
    return LIMIT / jnp.maximum(jnp.sqrt(square), LIMIT)


def stepped(master, new_mean, new_var):
    spread = new_var * VAR_SCALE
    spread = spread * lax.rsqrt(spread)
    return 0.998 * master - new_mean * MEAN_SCALE / (spread + 1e-08)


def weights_kernel(square_ref, plain_ref, master_ref, mean_ref, var_ref, out_ref):
    grad = plain_ref[...] * clip_factor(square_ref)
    new_mean = 0.9 * mean_ref[...] + 0.1 * grad
    new_var = 0.95 * var_ref[...] + 0.05 * grad * grad
    out_ref[...] = stepped(master_ref[...], new_mean, new_var).astype(jnp.bfloat16)


def state_kernel(square_ref, plain_ref, master_ref, mean_ref, var_ref, new_master_ref, new_mean_ref, new_var_ref):
    grad = plain_ref[...] * clip_factor(square_ref)
    new_mean = 0.9 * mean_ref[...] + 0.1 * grad
    new_var = 0.95 * var_ref[...] + 0.05 * grad * grad
    new_mean_ref[...] = new_mean
    new_var_ref[...] = new_var
    new_master_ref[...] = stepped(master_ref[...], new_mean, new_var)


def adamw(kernel, out_shape, square, plain, master, mean, var, skip):
    rows = pl.BlockSpec((STEP, WIDTH), lambda j: (j + skip, 0))
    count = BLOCK // STEP - skip
    return pl.pallas_call(
        kernel,
        out_shape=out_shape,
        grid=(count,),
        in_specs=[pl.BlockSpec(square.shape, lambda j: (0, 0, 0))] + [rows] * 4,
        out_specs=jax.tree.map(lambda _: pl.BlockSpec((STEP, WIDTH), lambda j: (j, 0)), out_shape),
        compiler_params=pltpu.CompilerParams(vmem_limit_bytes=VMEM_BYTES),
        cost_estimate=pl.CostEstimate(flops=20 * count * STEP * WIDTH, bytes_accessed=24 * count * STEP * WIDTH, transcendentals=count * STEP * WIDTH),
    )(square, plain, master, mean, var)


def pack_kernel(master_ref, mean_ref, var_ref, after_ref, out_ref):
    del after_ref
    master = master_ref[...]
    high = master.astype(jnp.bfloat16)
    out_ref[0] = high
    out_ref[1] = (master - high.astype(jnp.float32)).astype(jnp.bfloat16)
    out_ref[2] = mean_ref[...].astype(jnp.bfloat16)
    out_ref[3] = var_ref[...].astype(jnp.bfloat16)


def pack(master, mean, var, after):
    rows = pl.BlockSpec((STEP, WIDTH), lambda j: (j, 0))
    return pl.pallas_call(
        pack_kernel,
        out_shape=pltpu.HBM((4, PART, WIDTH), jnp.bfloat16),
        grid=(PART // STEP,),
        in_specs=[rows] * 3 + [pl.BlockSpec((1, 16, 128), lambda j: (0, 0, 0))],
        out_specs=pl.BlockSpec((4, STEP, WIDTH), lambda j: (0, j, 0)),
        compiler_params=pltpu.CompilerParams(vmem_limit_bytes=VMEM_BYTES),
        cost_estimate=pl.CostEstimate(flops=PART * WIDTH * 4, bytes_accessed=PART * WIDTH * 20, transcendentals=0),
    )(master, mean, var, after)


def wide_kernel(square_ref, packed_ref, plain_ref, out_ref):
    f32 = jnp.float32
    master = packed_ref[0, 0].astype(f32) + packed_ref[0, 1].astype(f32)
    grad = plain_ref[0].astype(f32) * clip_factor(square_ref)
    new_mean = 0.9 * packed_ref[0, 2].astype(f32) + 0.1 * grad
    new_var = 0.95 * packed_ref[0, 3].astype(f32) + 0.05 * grad * grad
    out_ref[...] = stepped(master, new_mean, new_var).astype(jnp.bfloat16)


def wide(square, packed, plain):
    sources = packed.shape[0]
    return pl.pallas_call(
        wide_kernel,
        out_shape=pltpu.HBM((BLOCK, D), jnp.bfloat16),
        grid=(sources,),
        in_specs=[
            pl.BlockSpec(square.shape, lambda j: (0, 0, 0)),
            pl.BlockSpec((1, 4, PART, WIDTH), lambda j: (j, 0, 0, 0)),
            pl.BlockSpec((1, PART, WIDTH), lambda j: (j, 0, 0)),
        ],
        out_specs=pl.BlockSpec((PART, WIDTH), lambda j: (0, j)),
        compiler_params=pltpu.CompilerParams(vmem_limit_bytes=VMEM_BYTES),
        cost_estimate=pl.CostEstimate(flops=20 * PART * D, bytes_accessed=12 * PART * D, transcendentals=PART * D),
    )(square, packed, plain)


def fill_kernel(rows_ref, given_ref, out_ref):
    del given_ref
    for j in range(rows_ref.shape[0]):
        out_ref[:, j * WIDTH : (j + 1) * WIDTH] = rows_ref[j]


def fill(rows, weights):
    count = 4
    sources = rows.shape[0] // count
    return pl.pallas_call(
        fill_kernel,
        out_shape=jax.ShapeDtypeStruct(weights.shape, weights.dtype),
        grid=(count,),
        in_specs=[pl.BlockSpec((sources, PART, WIDTH), lambda i: (i, 0, 0)), pl.BlockSpec(memory_space=pl.ANY)],
        out_specs=pl.BlockSpec((PART, sources * WIDTH), lambda i: (1, i)),
        input_output_aliases={1: 0},
        compiler_params=pltpu.CompilerParams(vmem_limit_bytes=VMEM_BYTES),
        cost_estimate=pl.CostEstimate(flops=0, bytes_accessed=4 * PART * D, transcendentals=0),
    )(rows, weights)


def on_device(grad_shards, hadamard_signs, scale_index, scale_table, master, mean_moment, var_moment):
    grad, scale_index, master, mean_moment, var_moment = map(in_hbm, (grad_shards[0], scale_index, master, mean_moment, var_moment))
    place = (lax.axis_index("dp") * 2 + (lax.axis_index("fsdp") & 1)).reshape(1)
    sign = in_hbm(hadamard_signs.reshape(1, WIDTH))
    hmat = in_hbm(jnp.asarray(hadamard(TILE)))
    terms, packed = reduce_scatter(place, scale_table, sign, grad, scale_index, hmat, functools.partial(pack, master, mean_moment, var_moment))
    packed = in_hbm(packed)
    plain, low, square = decode(place, scale_table, sign, terms, scale_index, hmat, packed, lax.axis_size("fsdp"))
    low = in_hbm(lax.all_gather(low, "fsdp"))
    square = total_squares(square)
    state = (square, plain, master, mean_moment, var_moment)
    rest = adamw(weights_kernel, pltpu.HBM((BLOCK - PART, WIDTH), jnp.bfloat16), *state, PART // STEP)
    rest = in_hbm(lax.all_gather(rest, "fsdp"))
    weights = fill(rest, wide(square, packed, low))
    new_state = adamw(state_kernel, (jax.ShapeDtypeStruct(master.shape, jnp.float32),) * 3, *state, 0)
    return *new_state, weights


def solution(mesh):
    return jax.shard_map(
        on_device,
        mesh=mesh,
        in_specs=(
            P("dp", None, "fsdp"),
            P("fsdp"),
            P("fsdp", None),
            P(),
            P("dp", "fsdp"),
            P("dp", "fsdp"),
            P("dp", "fsdp"),
        ),
        out_specs=(P("dp", "fsdp"), P("dp", "fsdp"), P("dp", "fsdp"), P("dp", None)),
        check_vma=False,
    )
```

```python
import functools
import math

import jax
import jax.numpy as jnp
import ml_dtypes
import numpy as np
from jax import lax
from jax.experimental import pallas as pl
from jax.experimental.pallas import tpu as pltpu
from jax.sharding import PartitionSpec as P

D = 6144
ROWS = 8192
TILE = 256
WIDTH = 768
TILES = WIDTH // TILE
SIDE = 4
BLOCK = 512
PART = 256
STEP = 128
RING0, RING1 = (2, 1), (3, 0)
LIMIT = 4.0 * math.sqrt(ROWS * D)
VMEM_BYTES = 14 * 1024 * 1024


def hadamard(length):
    index = np.arange(length)
    common_bits = index[:, None] & index[None, :]
    parity = np.zeros((length, length), np.int32)
    for bit_pos in range(length.bit_length() - 1):
        parity = parity ^ common_bits >> bit_pos & 1
    return (1 - 2 * parity).astype(ml_dtypes.bfloat16)


def hop(value, axis, step):
    pairs = []
    for device in range(128):
        x, z, core = device // 32, device // 8 % SIDE, device % 2
        if (axis == "first") == (core == 0):
            x = (x + step) % SIDE
        else:
            z = (z + step) % SIDE
        pairs.append((device, (x * SIDE + z) * 8 + device % 8))
    return lax.ppermute(value, ("dp", "fsdp"), pairs)


def in_hbm(value):
    return pltpu.with_memory_space_constraint(value, pltpu.HBM)


def row_scales(index_refs, table_ref, inverse):
    index = jnp.concatenate([ref[...] for ref in index_refs], axis=1)
    scale = jnp.zeros(index.shape, jnp.float32)
    for level in range(table_ref.shape[0]):
        scale = jnp.where(index == level, table_ref[level], scale)
    if inverse:
        scale = 1.0 / (math.sqrt(TILE) * scale)
    ones = jnp.ones((8 - index.shape[0], index.shape[1]), jnp.float32)
    return jnp.concatenate([scale, ones], axis=0).T


def encode_kernel(counts, ordered, place_ref, table_ref, sign_ref, hmat_ref, *refs):
    jobs = len(counts)
    inputs, out_refs = iter(refs[int(ordered) : -jobs]), refs[-jobs:]
    grad_refs, index_refs, arrived_refs = [], [], []
    for count in counts:
        grad_refs.append(next(inputs))
        index_refs.append(next(inputs))
        arrived_refs.append([next(inputs) for _ in range(count)])
    steps = row_scales(index_refs, table_ref, True)
    sign = (2 * sign_ref[...] - 1).astype(jnp.bfloat16)
    for tile in range(TILES):
        cols = slice(tile * TILE, (tile + 1) * TILE)
        signed = jnp.concatenate([ref[:, cols] for ref in grad_refs], axis=0) * sign[:, cols]
        rotated = jnp.dot(signed, hmat_ref[...], preferred_element_type=jnp.float32)
        codes = jnp.clip(rotated * steps[:, tile : tile + 1], -127.0, 127.0).astype(jnp.bfloat16)
        for job in range(jobs):
            code = codes[job * PART : (job + 1) * PART]
            if arrived_refs[job]:
                total = code.astype(jnp.float32)
                for ref in arrived_refs[job]:
                    total = total + ref[:, cols].astype(jnp.float32)
                code = total.astype(out_refs[job].dtype)
            out_refs[job][:, cols] = code


def block_at(place_ref, near, far):
    place = place_ref[0]
    x, z, core = place // (2 * SIDE), place // 2 % SIDE, place % 2
    x, z = x + jnp.where(core == 0, near, far), z + jnp.where(core == 0, far, near)
    return lax.rem(x, SIDE) * SIDE + lax.rem(z, SIDE)


def encode(place, table, sign, grad, index, hmat, grid, jobs, after=None):
    in_specs = [
        pl.BlockSpec(memory_space=pltpu.SMEM),
        pl.BlockSpec((1, WIDTH), lambda *_: (0, 0)),
        pl.BlockSpec((TILE, TILE), lambda *_: (0, 0)),
    ]
    operands, out_specs, out_shape = [table, sign, hmat], [], []
    if after is not None:
        in_specs.append(pl.BlockSpec((8, 128), lambda *_: (0, 0)))
        operands.append(after)
    parts = BLOCK // PART
    for near, far, arrived, spec, shape, dtype in jobs:
        rows = functools.partial(lambda near, far, i, j, place_ref: block_at(place_ref, near, far(i)) * parts + j, near, far)
        in_specs.append(pl.BlockSpec((PART, WIDTH), functools.partial(lambda rows, *at: (rows(*at), 0), rows)))
        in_specs.append(pl.BlockSpec((TILES, PART), functools.partial(lambda rows, *at: (0, rows(*at)), rows)))
        operands += [grad, index]
        for value, its_spec in arrived:
            in_specs.append(its_spec)
            operands.append(value)
        out_specs.append(spec)
        out_shape.append(jax.ShapeDtypeStruct(shape, dtype))
    blocks = len(jobs) * grid[0] * parts
    return pl.pallas_call(
        functools.partial(encode_kernel, [len(job[2]) for job in jobs], after is not None),
        out_shape=out_shape,
        grid_spec=pltpu.PrefetchScalarGridSpec(num_scalar_prefetch=1, grid=grid, in_specs=in_specs, out_specs=out_specs),
        compiler_params=pltpu.CompilerParams(vmem_limit_bytes=VMEM_BYTES),
        cost_estimate=pl.CostEstimate(flops=2 * blocks * PART * WIDTH * TILE, bytes_accessed=blocks * PART * WIDTH * 6, transcendentals=0),
    )(place, *operands)


def paired(ring):
    return lambda i: ring[0] + i * (ring[1] - ring[0])


def reduce_scatter(place, table, sign, grad, index, hmat, staged):
    code = functools.partial(encode, place, table, sign, grad, index, hmat)
    pair = ((2, BLOCK, WIDTH), jnp.bfloat16)
    both = pl.BlockSpec((None, PART, WIDTH), lambda i, j, place_ref: (i, j, 0))
    grid = (2, BLOCK // PART)

    def round_of(*plan):
        jobs = [(near, paired(ring), [(v, both) for v in arrived], both, *pair) for _, near, ring, arrived in plan]
        codes = code(grid, jobs)
        return [hop(v, "first", step) for v, (step, *_) in zip(codes, plan, strict=True)]

    up_far, down_far = round_of((1, 2, RING0, ()), (-1, 2, RING1, ()))
    up_own, down_own = round_of((1, 1, RING1, ()), (-1, 3, RING0, ()))
    single = pl.BlockSpec((PART, WIDTH), lambda i, j, place_ref: (j, 0))
    low = ((BLOCK, WIDTH), jnp.bfloat16)

    def of_slot(slot):
        return pl.BlockSpec((None, PART, WIDTH), lambda i, j, place_ref: (slot, j, 0))

    def sums_of(slot):
        plan = ((1, 1, RING0[slot], up_far), (-1, 3, RING1[slot], down_far))
        jobs = [(near, lambda i, far=far: far, [(v, of_slot(slot))], single, *low) for _, near, far, v in plan]
        return [hop(v, "first", step) for v, (step, *_) in zip(code((1, BLOCK // PART), jobs, staged), plan, strict=True)]

    def own_of(slot, up_sum, down_sum):
        plan = ((RING0[slot], up_sum, down_own), (RING1[slot], down_sum, up_own))
        jobs = []
        for far, whole, part in plan:
            shape = low if far else ((BLOCK, WIDTH), jnp.float32)
            jobs.append((0, lambda i, far=far: far, [(whole, single), (part, of_slot(slot))], single, *shape))
        values = code((1, BLOCK // PART), jobs)
        return [in_hbm(hop(v, "second", far)) if far else v for v, (far, *_) in zip(values, plan, strict=True)]

    early, late = sums_of(0), sums_of(1)
    two, three = own_of(0, *early)
    one, own = own_of(1, *late)
    return [own, two, one, three]


def decode_kernel(place_ref, table_ref, sign_ref, hmat_ref, own_ref, two_ref, one_ref, three_ref, index_ref, plain_ref, square_ref, sum_ref):
    f32 = jnp.float32

    @pl.when(pl.program_id(0) == 0)
    def _():
        sum_ref[...] = jnp.zeros_like(sum_ref)

    scales = row_scales([index_ref], table_ref, False) * (1.0 / math.sqrt(TILE))
    sign = (2 * sign_ref[...] - 1).astype(f32)
    square = sum_ref[...]
    for tile in range(TILES):
        cols = slice(tile * TILE, (tile + 1) * TILE)
        value = own_ref[:, cols] + two_ref[:, cols].astype(f32) + one_ref[:, cols].astype(f32) + three_ref[:, cols].astype(f32)
        plain = jnp.zeros(value.shape, f32)
        for _ in range(3):
            piece = value.astype(jnp.bfloat16)
            plain = plain + jnp.dot(piece, hmat_ref[...], preferred_element_type=f32)
            value = value - piece.astype(f32)
        plain = plain * scales[:, tile : tile + 1] * sign[:, cols]
        plain_ref[:, cols] = plain
        parts = jnp.sum((plain * plain).reshape(-1, 8, TILE), axis=0)
        square = square + parts[:, :128] + parts[:, 128:]
    sum_ref[...] = square
    square_ref[...] = jnp.broadcast_to(square, square_ref.shape)


def decode(place, table, sign, terms, index, hmat, copies):
    parts = BLOCK // PART
    single = pl.BlockSpec((PART, WIDTH), lambda j, place_ref: (j, 0))
    return pl.pallas_call(
        decode_kernel,
        out_shape=(
            jax.ShapeDtypeStruct((BLOCK, WIDTH), jnp.float32),
            pltpu.HBM((copies, 8, 128), jnp.float32),
        ),
        grid_spec=pltpu.PrefetchScalarGridSpec(
            num_scalar_prefetch=1,
            grid=(parts,),
            in_specs=[
                pl.BlockSpec(memory_space=pltpu.SMEM),
                pl.BlockSpec((1, WIDTH), lambda j, place_ref: (0, 0)),
                pl.BlockSpec((TILE, TILE), lambda j, place_ref: (0, 0)),
                *[single] * 4,
                pl.BlockSpec((TILES, PART), lambda j, place_ref: (0, block_at(place_ref, 0, 0) * parts + j)),
            ],
            out_specs=(
                single,
                pl.BlockSpec((copies, 8, 128), lambda j, place_ref: (0, 0, 0)),
            ),
            scratch_shapes=[pltpu.VMEM((8, 128), jnp.float32)],
        ),
        compiler_params=pltpu.CompilerParams(vmem_limit_bytes=VMEM_BYTES),
        cost_estimate=pl.CostEstimate(flops=6 * 512 * WIDTH * TILE, bytes_accessed=512 * WIDTH * 14, transcendentals=0),
    )(place, table, sign, hmat, *terms, index)


def total_squares(square):
    square = jnp.sum(lax.all_to_all(square, "fsdp", 0, 0), axis=0)
    copies = jnp.broadcast_to(square, (lax.axis_size("dp"), *square.shape))
    return lax.all_to_all(copies, "dp", 0, 0)


MEAN_SCALE = 0.02 / (1.0 - 0.9**10)
VAR_SCALE = 1.0 / (1.0 - 0.95**10)


def clip_factor(square_ref):
    square = jnp.sum(square_ref[...], axis=0)
    square = jnp.sum(jnp.sum(square, axis=0, keepdims=True), axis=1, keepdims=True)
    return LIMIT / jnp.maximum(jnp.sqrt(square), LIMIT)


def stepped(master, new_mean, new_var):
    spread = new_var * VAR_SCALE
    spread = spread * lax.rsqrt(spread)
    return 0.998 * master - new_mean * MEAN_SCALE / (spread + 1e-08)


def weights_kernel(square_ref, plain_ref, master_ref, mean_ref, var_ref, out_ref):
    grad = plain_ref[...] * clip_factor(square_ref)
    new_mean = 0.9 * mean_ref[...] + 0.1 * grad
    new_var = 0.95 * var_ref[...] + 0.05 * grad * grad
    out_ref[...] = stepped(master_ref[...], new_mean, new_var).astype(jnp.bfloat16)


def state_kernel(square_ref, plain_ref, master_ref, mean_ref, var_ref, new_master_ref, new_mean_ref, new_var_ref):
    grad = plain_ref[...] * clip_factor(square_ref)
    new_mean = 0.9 * mean_ref[...] + 0.1 * grad
    new_var = 0.95 * var_ref[...] + 0.05 * grad * grad
    new_mean_ref[...] = new_mean
    new_var_ref[...] = new_var
    new_master_ref[...] = stepped(master_ref[...], new_mean, new_var)


def adamw(kernel, out_shape, square, plain, master, mean, var):
    rows = pl.BlockSpec((STEP, WIDTH), lambda j: (j, 0))
    return pl.pallas_call(
        kernel,
        out_shape=out_shape,
        grid=(BLOCK // STEP,),
        in_specs=[pl.BlockSpec(square.shape, lambda j: (0, 0, 0))] + [rows] * 4,
        out_specs=jax.tree.map(lambda _: rows, out_shape),
        compiler_params=pltpu.CompilerParams(vmem_limit_bytes=VMEM_BYTES),
        cost_estimate=pl.CostEstimate(flops=20 * BLOCK * WIDTH, bytes_accessed=24 * BLOCK * WIDTH, transcendentals=BLOCK * WIDTH),
    )(square, plain, master, mean, var)


def stage_kernel(*refs):
    for source, target in zip(refs[:3], refs[3:6], strict=True):
        target[...] = source[...]
    refs[6][...] = jnp.zeros_like(refs[6])


def stage(*state):
    rows = pl.BlockSpec((STEP, WIDTH), lambda j: (j, 0))
    return pl.pallas_call(
        stage_kernel,
        out_shape=[pltpu.VMEM(v.shape, v.dtype) for v in state] + [jax.ShapeDtypeStruct((8, 128), jnp.float32)],
        grid=(BLOCK // STEP,),
        in_specs=[rows] * 3,
        out_specs=[rows] * 3 + [pl.BlockSpec((8, 128), lambda j: (0, 0))],
        compiler_params=pltpu.CompilerParams(vmem_limit_bytes=VMEM_BYTES),
        cost_estimate=pl.CostEstimate(flops=0, bytes_accessed=24 * BLOCK * WIDTH, transcendentals=0),
    )(*state)


def after(value, first):
    anywhere = pl.BlockSpec(memory_space=pl.ANY)
    return pl.pallas_call(
        lambda *_: None,
        out_shape=jax.ShapeDtypeStruct(value.shape, value.dtype),
        in_specs=[anywhere, anywhere],
        out_specs=anywhere,
        input_output_aliases={0: 0},
        compiler_params=pltpu.CompilerParams(vmem_limit_bytes=VMEM_BYTES),
    )(value, first)


def fill_kernel(places, at_ref, *refs):
    count = len(places)
    out_ref, tile_ref, sems = refs[-3:]
    tile_ref[...] = jnp.zeros_like(tile_ref)
    chip, core = at_ref[0] // 2, at_ref[0] % 2
    copies = []
    for j, (step, swapped) in enumerate(places):
        source = (chip + SIDE - step + 2 * step * core) % SIDE
        column = pl.multiple_of((source * 2 + (1 - core if swapped else core)) * WIDTH, WIDTH)
        target = out_ref.at[:, pl.ds(column, WIDTH)]
        copies.append(pltpu.make_async_copy(refs[j], target, sems.at[j]))
    for copy in copies:
        copy.start()
    for copy in copies:
        copy.wait()


def fill(at, places, blocks, weights=None):
    anywhere = pl.BlockSpec(memory_space=pl.ANY)
    whole = pl.BlockSpec(blocks[0].shape, lambda: (0, 0))
    given = [] if weights is None else [weights]
    return pl.pallas_call(
        functools.partial(fill_kernel, places),
        out_shape=(pltpu.HBM((BLOCK, D), jnp.bfloat16), jax.ShapeDtypeStruct((8, 128), jnp.float32)),
        in_specs=[pl.BlockSpec(memory_space=pltpu.SMEM)] + [whole] * len(blocks) + [anywhere] * len(given),
        out_specs=(anywhere, pl.BlockSpec((8, 128), lambda: (0, 0))),
        scratch_shapes=[pltpu.SemaphoreType.DMA((len(blocks),))],
        input_output_aliases={len(blocks) + 1: 0} if given else {},
        compiler_params=pltpu.CompilerParams(vmem_limit_bytes=VMEM_BYTES),
        cost_estimate=pl.CostEstimate(flops=0, bytes_accessed=4 * len(blocks) * blocks[0].size, transcendentals=0),
    )(at, *blocks, *given)


def along_y(value):
    pairs = [(y * 2 + core, (y + 1 - 2 * core) % SIDE * 2 + core) for y in range(SIDE) for core in range(2)]
    return lax.ppermute(value, "fsdp", pairs)


def to_other_core(value):
    return lax.ppermute(value, "fsdp", [(i, i ^ 1) for i in range(8)])


def gather(low, state):
    at = lax.axis_index("fsdp").reshape(1)
    one = along_y(low)
    other = to_other_core(low)
    one_other = along_y(other)
    one = after(one, state)
    two = along_y(one)
    one_swapped = to_other_core(one)
    other_swapped = to_other_core(one_other)
    near = ((0, False), (0, True), (1, False), (1, True), (-1, True), (-1, False))
    weights, filled = fill(at, near, (low, other, one, one_other, one_swapped, other_swapped))
    two = after(two, filled)
    two_swapped = to_other_core(two)
    return fill(at, ((2, False), (2, True)), (two, two_swapped), weights)[0]


def on_device(grad_shards, hadamard_signs, scale_index, scale_table, master, mean_moment, var_moment):
    grad, scale_index, master, mean_moment, var_moment = map(in_hbm, (grad_shards[0], scale_index, master, mean_moment, var_moment))
    scale_table = in_hbm(scale_table)
    place = (lax.axis_index("dp") * 2 + (lax.axis_index("fsdp") & 1)).reshape(1)
    sign = in_hbm(hadamard_signs.reshape(1, WIDTH))
    hmat = in_hbm(jnp.asarray(hadamard(TILE)))
    *state, staged = stage(master, mean_moment, var_moment)
    terms = reduce_scatter(place, scale_table, sign, grad, scale_index, hmat, staged)
    plain, square = decode(place, scale_table, sign, terms, scale_index, hmat, lax.axis_size("fsdp"))
    square = total_squares(square)
    low = adamw(weights_kernel, jax.ShapeDtypeStruct((BLOCK, WIDTH), jnp.bfloat16), square, plain, *state)
    new_state = adamw(state_kernel, (jax.ShapeDtypeStruct(master.shape, jnp.float32),) * 3, square, plain, *state)
    return *new_state, gather(low, new_state[0])


def solution(mesh):
    return jax.shard_map(
        on_device,
        mesh=mesh,
        in_specs=(
            P("dp", None, "fsdp"),
            P("fsdp"),
            P("fsdp", None),
            P(),
            P("dp", "fsdp"),
            P("dp", "fsdp"),
            P("dp", "fsdp"),
        ),
        out_specs=(P("dp", "fsdp"), P("dp", "fsdp"), P("dp", "fsdp"), P("dp", None)),
        check_vma=False,
    )
```

```python
import functools
import math

import jax
import jax.numpy as jnp
import ml_dtypes
import numpy as np
from jax import lax
from jax.experimental import pallas as pl
from jax.experimental.pallas import tpu as pltpu
from jax.sharding import PartitionSpec as P

D = 6144
ROWS = 8192
TILE = 256
WIDTH = 768
TILES = WIDTH // TILE
SIDE = 4
BLOCK = 512
PART = 256
STEP = 128
RING0, RING1 = (2, 1), (3, 0)
LIMIT = 4.0 * math.sqrt(ROWS * D)
VMEM_BYTES = 14 * 1024 * 1024


def hadamard(length):
    index = np.arange(length)
    common_bits = index[:, None] & index[None, :]
    parity = np.zeros((length, length), np.int32)
    for bit_pos in range(length.bit_length() - 1):
        parity = parity ^ common_bits >> bit_pos & 1
    return (1 - 2 * parity).astype(ml_dtypes.bfloat16)


def hop(value, axis, step):
    pairs = []
    for device in range(128):
        x, z, core = device // 32, device // 8 % SIDE, device % 2
        if (axis == "first") == (core == 0):
            x = (x + step) % SIDE
        else:
            z = (z + step) % SIDE
        pairs.append((device, (x * SIDE + z) * 8 + device % 8))
    return lax.ppermute(value, ("dp", "fsdp"), pairs)


def in_hbm(value):
    return pltpu.with_memory_space_constraint(value, pltpu.HBM)


def in_vmem(value):
    return pltpu.with_memory_space_constraint(value, pltpu.VMEM)


def row_scales(index_refs, table_ref, inverse):
    index = jnp.concatenate([ref[...] for ref in index_refs], axis=1)
    scale = jnp.zeros(index.shape, jnp.float32)
    for level in range(table_ref.shape[0]):
        scale = jnp.where(index == level, table_ref[level], scale)
    if inverse:
        scale = 1.0 / (math.sqrt(TILE) * scale)
    ones = jnp.ones((8 - index.shape[0], index.shape[1]), jnp.float32)
    return jnp.concatenate([scale, ones], axis=0).T


def encode_kernel(counts, ordered, place_ref, table_ref, sign_ref, hmat_ref, *refs):
    jobs = len(counts)
    inputs, out_refs = iter(refs[int(ordered) : -jobs]), refs[-jobs:]
    grad_refs, index_refs, arrived_refs = [], [], []
    for count in counts:
        grad_refs.append(next(inputs))
        index_refs.append(next(inputs))
        arrived_refs.append([next(inputs) for _ in range(count)])
    steps = row_scales(index_refs, table_ref, True)
    sign = (2 * sign_ref[...] - 1).astype(jnp.bfloat16)
    for tile in range(TILES):
        cols = slice(tile * TILE, (tile + 1) * TILE)
        signed = jnp.concatenate([ref[:, cols] for ref in grad_refs], axis=0) * sign[:, cols]
        rotated = jnp.dot(signed, hmat_ref[...], preferred_element_type=jnp.float32)
        codes = jnp.clip(rotated * steps[:, tile : tile + 1], -127.0, 127.0).astype(jnp.bfloat16)
        for job in range(jobs):
            code = codes[job * PART : (job + 1) * PART]
            if arrived_refs[job]:
                total = code.astype(jnp.float32)
                for ref in arrived_refs[job]:
                    total = total + ref[:, cols].astype(jnp.float32)
                code = total.astype(out_refs[job].dtype)
            out_refs[job][:, cols] = code


def block_at(place_ref, near, far):
    place = place_ref[0]
    x, z, core = place // (2 * SIDE), place // 2 % SIDE, place % 2
    x, z = x + jnp.where(core == 0, near, far), z + jnp.where(core == 0, far, near)
    return lax.rem(x, SIDE) * SIDE + lax.rem(z, SIDE)


def encode(place, table, sign, grad, index, hmat, grid, jobs, after=None):
    in_specs = [
        pl.BlockSpec(memory_space=pltpu.SMEM),
        pl.BlockSpec((1, WIDTH), lambda *_: (0, 0)),
        pl.BlockSpec((TILE, TILE), lambda *_: (0, 0)),
    ]
    operands, out_specs, out_shape = [table, sign, hmat], [], []
    if after is not None:
        in_specs.append(pl.BlockSpec((8, 128), lambda *_: (0, 0)))
        operands.append(after)
    parts = BLOCK // PART
    for near, far, arrived, spec, shape, dtype in jobs:
        rows = functools.partial(lambda near, far, i, j, place_ref: block_at(place_ref, near, far(i)) * parts + j, near, far)
        in_specs.append(pl.BlockSpec((PART, WIDTH), functools.partial(lambda rows, *at: (rows(*at), 0), rows)))
        in_specs.append(pl.BlockSpec((TILES, PART), functools.partial(lambda rows, *at: (0, rows(*at)), rows)))
        operands += [grad, index]
        for value, its_spec in arrived:
            in_specs.append(its_spec)
            operands.append(value)
        out_specs.append(spec)
        out_shape.append(jax.ShapeDtypeStruct(shape, dtype))
    blocks = len(jobs) * grid[0] * parts
    return pl.pallas_call(
        functools.partial(encode_kernel, [len(job[2]) for job in jobs], after is not None),
        out_shape=out_shape,
        grid_spec=pltpu.PrefetchScalarGridSpec(num_scalar_prefetch=1, grid=grid, in_specs=in_specs, out_specs=out_specs),
        compiler_params=pltpu.CompilerParams(vmem_limit_bytes=VMEM_BYTES),
        cost_estimate=pl.CostEstimate(flops=0, bytes_accessed=0, transcendentals=0),
    )(place, *operands)


def paired(ring):
    return lambda i: ring[0] + i * (ring[1] - ring[0])


def reduce_scatter(place, table, sign, grad, index, hmat, staged):
    code = functools.partial(encode, place, table, sign, grad, index, hmat)
    pair = ((2, BLOCK, WIDTH), jnp.bfloat16)
    both = pl.BlockSpec((None, PART, WIDTH), lambda i, j, place_ref: (i, j, 0))
    grid = (2, BLOCK // PART)

    def round_of(*plan):
        jobs = [(near, paired(ring), [(v, both) for v in arrived], both, *pair) for _, near, ring, arrived in plan]
        codes = code(grid, jobs)
        return [hop(v, "first", step) for v, (step, *_) in zip(codes, plan, strict=True)]

    up_far, down_far = round_of((1, 2, RING0, ()), (-1, 2, RING1, ()))
    up_own, down_own = round_of((1, 1, RING1, ()), (-1, 3, RING0, ()))
    single = pl.BlockSpec((PART, WIDTH), lambda i, j, place_ref: (j, 0))
    low = ((BLOCK, WIDTH), jnp.bfloat16)

    def of_slot(slot):
        return pl.BlockSpec((None, PART, WIDTH), lambda i, j, place_ref: (slot, j, 0))

    def sums_of(slot):
        plan = ((1, 1, RING0[slot], up_far), (-1, 3, RING1[slot], down_far))
        jobs = [(near, lambda i, far=far: far, [(v, of_slot(slot))], single, *low) for _, near, far, v in plan]
        return [hop(v, "first", step) for v, (step, *_) in zip(code((1, BLOCK // PART), jobs, staged), plan, strict=True)]

    def own_of(slot, *rings):
        plan, jobs = [], []
        for ring, whole in rings:
            far, part = (RING0[slot], down_own) if ring == 0 else (RING1[slot], up_own)
            shape = low if far else ((BLOCK, WIDTH), jnp.float32)
            jobs.append((0, lambda i, far=far: far, [(whole, single), (part, of_slot(slot))], single, *shape))
            plan.append(far)
        values = code((1, BLOCK // PART), jobs)
        return [in_vmem(hop(v, "second", far)) if far else v for v, far in zip(values, plan, strict=True)]

    early_up, early_down = sums_of(0)
    late_up, late_down = sums_of(1)
    two, three = own_of(0, (0, early_up), (1, early_down))
    (one,) = own_of(1, (0, late_up))
    (own,) = own_of(1, (1, late_down))
    return [own, two, one, three]


def decode_kernel(place_ref, table_ref, sign_ref, hmat_ref, own_ref, two_ref, one_ref, three_ref, index_ref, plain_ref, square_ref, sum_ref):
    f32 = jnp.float32

    @pl.when(pl.program_id(0) == 0)
    def _():
        sum_ref[...] = jnp.zeros_like(sum_ref)

    scales = row_scales([index_ref], table_ref, False) * (1.0 / math.sqrt(TILE))
    sign = (2 * sign_ref[...] - 1).astype(f32)
    square = sum_ref[...]
    for tile in range(TILES):
        cols = slice(tile * TILE, (tile + 1) * TILE)
        value = own_ref[:, cols] + two_ref[:, cols].astype(f32) + one_ref[:, cols].astype(f32) + three_ref[:, cols].astype(f32)
        plain = jnp.zeros(value.shape, f32)
        for _ in range(3):
            piece = value.astype(jnp.bfloat16)
            plain = plain + jnp.dot(piece, hmat_ref[...], preferred_element_type=f32)
            value = value - piece.astype(f32)
        plain = plain * scales[:, tile : tile + 1] * sign[:, cols]
        plain_ref[:, cols] = plain
        parts = jnp.sum((plain * plain).reshape(-1, 8, TILE), axis=0)
        square = square + parts[:, :128] + parts[:, 128:]
    sum_ref[...] = square
    square_ref[...] = jnp.broadcast_to(square, square_ref.shape)


def decode(place, table, sign, terms, index, hmat, copies):
    parts = BLOCK // PART
    single = pl.BlockSpec((PART, WIDTH), lambda j, place_ref: (j, 0))
    return pl.pallas_call(
        decode_kernel,
        out_shape=(
            pltpu.HBM((BLOCK, WIDTH), jnp.float32),
            pltpu.HBM((copies, 8, 128), jnp.float32),
        ),
        grid_spec=pltpu.PrefetchScalarGridSpec(
            num_scalar_prefetch=1,
            grid=(parts,),
            in_specs=[
                pl.BlockSpec(memory_space=pltpu.SMEM),
                pl.BlockSpec((1, WIDTH), lambda j, place_ref: (0, 0)),
                pl.BlockSpec((TILE, TILE), lambda j, place_ref: (0, 0)),
                *[single] * 4,
                pl.BlockSpec((TILES, PART), lambda j, place_ref: (0, block_at(place_ref, 0, 0) * parts + j)),
            ],
            out_specs=(
                single,
                pl.BlockSpec((copies, 8, 128), lambda j, place_ref: (0, 0, 0)),
            ),
            scratch_shapes=[pltpu.VMEM((8, 128), jnp.float32)],
        ),
        compiler_params=pltpu.CompilerParams(vmem_limit_bytes=VMEM_BYTES),
        cost_estimate=pl.CostEstimate(flops=0, bytes_accessed=0, transcendentals=0),
    )(place, table, sign, hmat, *terms, index)


def total_squares(square):
    square = jnp.sum(lax.all_to_all(square, "fsdp", 0, 0), axis=0)
    copies = jnp.broadcast_to(square, (lax.axis_size("dp"), *square.shape))
    return lax.all_to_all(copies, "dp", 0, 0)


MEAN_SCALE = 0.02 / (1.0 - 0.9**10)
VAR_SCALE = 1.0 / (1.0 - 0.95**10)


def clip_factor(square_ref):
    square = jnp.sum(square_ref[...], axis=0)
    square = jnp.sum(jnp.sum(square, axis=0, keepdims=True), axis=1, keepdims=True)
    return LIMIT / jnp.maximum(jnp.sqrt(square), LIMIT)


def stepped(master, new_mean, new_var):
    spread = new_var * VAR_SCALE
    spread = spread * lax.rsqrt(spread)
    return 0.998 * master - new_mean * MEAN_SCALE / (spread + 1e-08)


def weights_kernel(square_ref, plain_ref, master_ref, mean_ref, var_ref, out_ref):
    grad = plain_ref[...] * clip_factor(square_ref)
    new_mean = 0.9 * mean_ref[...] + 0.1 * grad
    new_var = 0.95 * var_ref[...] + 0.05 * grad * grad
    out_ref[...] = stepped(master_ref[...], new_mean, new_var).astype(jnp.bfloat16)


def state_kernel(square_ref, plain_ref, master_ref, mean_ref, var_ref, new_master_ref, new_mean_ref, new_var_ref):
    grad = plain_ref[...] * clip_factor(square_ref)
    new_mean = 0.9 * mean_ref[...] + 0.1 * grad
    new_var = 0.95 * var_ref[...] + 0.05 * grad * grad
    new_mean_ref[...] = new_mean
    new_var_ref[...] = new_var
    new_master_ref[...] = stepped(master_ref[...], new_mean, new_var)


def adamw(kernel, out_shape, square, plain, master, mean, var):
    rows = pl.BlockSpec((STEP, WIDTH), lambda j: (j, 0))
    return pl.pallas_call(
        kernel,
        out_shape=out_shape,
        grid=(BLOCK // STEP,),
        in_specs=[pl.BlockSpec(square.shape, lambda j: (0, 0, 0))] + [rows] * 4,
        out_specs=jax.tree.map(lambda _: rows, out_shape),
        compiler_params=pltpu.CompilerParams(vmem_limit_bytes=VMEM_BYTES),
        cost_estimate=pl.CostEstimate(flops=0, bytes_accessed=0, transcendentals=0),
    )(square, plain, master, mean, var)


def stage_kernel(*refs):
    for source, target in zip(refs[:2], refs[2:4], strict=True):
        target[...] = source[...]
    refs[4][...] = jnp.zeros_like(refs[4])


def stage(*state):
    rows = pl.BlockSpec((STEP, WIDTH), lambda j: (j, 0))
    return pl.pallas_call(
        stage_kernel,
        out_shape=[pltpu.VMEM(v.shape, v.dtype) for v in state] + [jax.ShapeDtypeStruct((8, 128), jnp.float32)],
        grid=(BLOCK // STEP,),
        in_specs=[rows] * 2,
        out_specs=[rows] * 2 + [pl.BlockSpec((8, 128), lambda j: (0, 0))],
        compiler_params=pltpu.CompilerParams(vmem_limit_bytes=VMEM_BYTES),
        cost_estimate=pl.CostEstimate(flops=0, bytes_accessed=0, transcendentals=0),
    )(*state)


def after(value, first):
    anywhere = pl.BlockSpec(memory_space=pl.ANY)
    return pl.pallas_call(
        lambda *_: None,
        out_shape=jax.ShapeDtypeStruct(value.shape, value.dtype),
        in_specs=[anywhere, anywhere],
        out_specs=anywhere,
        input_output_aliases={0: 0},
        compiler_params=pltpu.CompilerParams(vmem_limit_bytes=VMEM_BYTES),
    )(value, first)


def fill_kernel(places, at_ref, *refs):
    count = len(places)
    out_ref, tile_ref, sems = refs[-3:]
    tile_ref[...] = jnp.zeros_like(tile_ref)
    chip, core = at_ref[0] // 2, at_ref[0] % 2
    copies = []
    for j, (step, swapped, row) in enumerate(places):
        source = (chip + SIDE - step + 2 * step * core) % SIDE
        column = pl.multiple_of((source * 2 + (1 - core if swapped else core)) * WIDTH, WIDTH)
        target = out_ref.at[pl.ds(row, refs[j].shape[0]), pl.ds(column, WIDTH)]
        copies.append(pltpu.make_async_copy(refs[j], target, sems.at[j]))
    for copy in copies:
        copy.start()
    for copy in copies:
        copy.wait()


def fill(at, places, blocks, weights=None):
    anywhere = pl.BlockSpec(memory_space=pl.ANY)
    given = [] if weights is None else [weights]
    return pl.pallas_call(
        functools.partial(fill_kernel, places),
        out_shape=(pltpu.HBM((BLOCK, D), jnp.bfloat16), jax.ShapeDtypeStruct((8, 128), jnp.float32)),
        in_specs=[pl.BlockSpec(memory_space=pltpu.SMEM)] + [pl.BlockSpec(v.shape, lambda: (0, 0)) for v in blocks] + [anywhere] * len(given),
        out_specs=(anywhere, pl.BlockSpec((8, 128), lambda: (0, 0))),
        scratch_shapes=[pltpu.SemaphoreType.DMA((len(blocks),))],
        input_output_aliases={len(blocks) + 1: 0} if given else {},
        compiler_params=pltpu.CompilerParams(vmem_limit_bytes=VMEM_BYTES),
        cost_estimate=pl.CostEstimate(flops=0, bytes_accessed=0, transcendentals=0),
    )(at, *blocks, *given)


def along_y(value):
    pairs = [(y * 2 + core, (y + 1 - 2 * core) % SIDE * 2 + core) for y in range(SIDE) for core in range(2)]
    return lax.ppermute(value, "fsdp", pairs)


def to_other_core(value):
    return lax.ppermute(value, "fsdp", [(i, i ^ 1) for i in range(8)])


def gather(low, state):
    at = lax.axis_index("fsdp").reshape(1)
    one = along_y(low)
    other = to_other_core(low)
    one_other = along_y(other)
    one = after(one, state)
    two = along_y(one)
    one_swapped = to_other_core(one)
    halves = [to_other_core(one_other[row : row + PART]) for row in (0, PART)]
    near = ((0, False, 0), (0, True, 0), (1, False, 0), (1, True, 0), (-1, True, 0), (-1, False, 0), (-1, False, PART))
    weights, filled = fill(at, near, (low, other, one, one_other, one_swapped, *halves))
    two = after(two, filled)
    two_swapped = to_other_core(two)
    return fill(at, ((2, False, 0), (2, True, 0)), (two, two_swapped), weights)[0]


def on_device(grad_shards, hadamard_signs, scale_index, scale_table, master, mean_moment, var_moment):
    grad, scale_index, master, mean_moment, var_moment = map(in_hbm, (grad_shards[0], scale_index, master, mean_moment, var_moment))
    scale_table = in_hbm(scale_table)
    place = (lax.axis_index("dp") * 2 + (lax.axis_index("fsdp") & 1)).reshape(1)
    sign = in_hbm(hadamard_signs.reshape(1, WIDTH))
    hmat = in_hbm(jnp.asarray(hadamard(TILE)))
    *state, staged = stage(master, mean_moment)
    state.append(var_moment)
    terms = reduce_scatter(place, scale_table, sign, grad, scale_index, hmat, staged)
    plain, square = decode(place, scale_table, sign, terms, scale_index, hmat, lax.axis_size("fsdp"))
    square = total_squares(square)
    low = adamw(weights_kernel, jax.ShapeDtypeStruct((BLOCK, WIDTH), jnp.bfloat16), square, in_hbm(plain), *state)
    new_state = adamw(state_kernel, (jax.ShapeDtypeStruct(master.shape, jnp.float32),) * 3, square, in_hbm(plain), *state)
    return *new_state, gather(low, in_hbm(new_state[0]))


def solution(mesh):
    return jax.shard_map(
        on_device,
        mesh=mesh,
        in_specs=(
            P("dp", None, "fsdp"),
            P("fsdp"),
            P("fsdp", None),
            P(),
            P("dp", "fsdp"),
            P("dp", "fsdp"),
            P("dp", "fsdp"),
        ),
        out_specs=(P("dp", "fsdp"), P("dp", "fsdp"), P("dp", "fsdp"), P("dp", None)),
        check_vma=False,
    )
```

```python
import functools
import math

import jax
import jax.numpy as jnp
import ml_dtypes
import numpy as np
from jax import lax
from jax.experimental import pallas as pl
from jax.experimental.pallas import tpu as pltpu
from jax.sharding import PartitionSpec as P

D = 6144
ROWS = 8192
TILE = 256
WIDTH = 768
TILES = WIDTH // TILE
SIDE = 4
BLOCK = 512
PART = 256
STEP = 128
RING0, RING1 = (2, 1), (3, 0)
LIMIT = 4.0 * math.sqrt(ROWS * D)
VMEM_BYTES = 14 * 1024 * 1024


def hadamard(length):
    index = np.arange(length)
    common_bits = index[:, None] & index[None, :]
    parity = np.zeros((length, length), np.int32)
    for bit_pos in range(length.bit_length() - 1):
        parity = parity ^ common_bits >> bit_pos & 1
    return (1 - 2 * parity).astype(ml_dtypes.bfloat16)


def hop(value, axis, step):
    pairs = []
    for device in range(128):
        x, z, core = device // 32, device // 8 % SIDE, device % 2
        if (axis == "first") == (core == 0):
            x = (x + step) % SIDE
        else:
            z = (z + step) % SIDE
        pairs.append((device, (x * SIDE + z) * 8 + device % 8))
    return lax.ppermute(value, ("dp", "fsdp"), pairs)


def in_hbm(value):
    return pltpu.with_memory_space_constraint(value, pltpu.HBM)


def in_vmem(value):
    return pltpu.with_memory_space_constraint(value, pltpu.VMEM)


def row_scales(index_refs, table_ref, inverse):
    index = jnp.concatenate([ref[...] for ref in index_refs], axis=1)
    scale = jnp.zeros(index.shape, jnp.float32)
    for level in range(table_ref.shape[0]):
        scale = jnp.where(index == level, table_ref[level], scale)
    if inverse:
        scale = 1.0 / (math.sqrt(TILE) * scale)
    ones = jnp.ones((8 - index.shape[0], index.shape[1]), jnp.float32)
    return jnp.concatenate([scale, ones], axis=0).T


def encode_kernel(counts, ordered, place_ref, table_ref, sign_ref, hmat_ref, *refs):
    jobs = len(counts)
    inputs, out_refs = iter(refs[int(ordered) : -jobs]), refs[-jobs:]
    grad_refs, index_refs, arrived_refs = [], [], []
    for count in counts:
        grad_refs.append(next(inputs))
        index_refs.append(next(inputs))
        arrived_refs.append([next(inputs) for _ in range(count)])
    steps = row_scales(index_refs, table_ref, True)
    sign = (2 * sign_ref[...] - 1).reshape(1, WIDTH).astype(jnp.bfloat16)
    for tile in range(TILES):
        cols = slice(tile * TILE, (tile + 1) * TILE)
        signed = jnp.concatenate([ref[:, cols] for ref in grad_refs], axis=0) * sign[:, cols]
        rotated = jnp.dot(signed, hmat_ref[...], preferred_element_type=jnp.float32)
        codes = jnp.clip(rotated * steps[:, tile : tile + 1], -127.0, 127.0).astype(jnp.bfloat16)
        for job in range(jobs):
            code = codes[job * PART : (job + 1) * PART]
            if arrived_refs[job]:
                total = code.astype(jnp.float32)
                for ref in arrived_refs[job]:
                    total = total + ref[:, cols].astype(jnp.float32)
                code = total.astype(out_refs[job].dtype)
            out_refs[job][:, cols] = code


def block_at(place_ref, near, far):
    place = place_ref[0]
    x, z, core = place // (2 * SIDE), place // 2 % SIDE, place % 2
    x, z = x + jnp.where(core == 0, near, far), z + jnp.where(core == 0, far, near)
    return lax.rem(x, SIDE) * SIDE + lax.rem(z, SIDE)


def encode(place, table, sign, grad, index, hmat, grid, jobs, after=None):
    in_specs = [
        pl.BlockSpec(memory_space=pltpu.SMEM),
        pl.BlockSpec((WIDTH,), lambda *_: (0,)),
        pl.BlockSpec((TILE, TILE), lambda *_: (0, 0)),
    ]
    operands, out_specs, out_shape = [table, sign, hmat], [], []
    if after is not None:
        in_specs.append(pl.BlockSpec((8, 128), lambda *_: (0, 0)))
        operands.append(after)
    parts = BLOCK // PART
    for near, far, arrived, spec, shape, dtype in jobs:
        rows = functools.partial(lambda near, far, i, j, place_ref: block_at(place_ref, near, far(i)) * parts + j, near, far)
        in_specs.append(pl.BlockSpec((PART, WIDTH), functools.partial(lambda rows, *at: (rows(*at), 0), rows)))
        in_specs.append(pl.BlockSpec((TILES, PART), functools.partial(lambda rows, *at: (0, rows(*at)), rows)))
        operands += [grad, index]
        for value, its_spec in arrived:
            in_specs.append(its_spec)
            operands.append(value)
        out_specs.append(spec)
        out_shape.append(jax.ShapeDtypeStruct(shape, dtype))
    blocks = len(jobs) * grid[0] * parts
    return pl.pallas_call(
        functools.partial(encode_kernel, [len(job[2]) for job in jobs], after is not None),
        out_shape=out_shape,
        grid_spec=pltpu.PrefetchScalarGridSpec(num_scalar_prefetch=1, grid=grid, in_specs=in_specs, out_specs=out_specs),
        compiler_params=pltpu.CompilerParams(vmem_limit_bytes=VMEM_BYTES),
        cost_estimate=pl.CostEstimate(flops=0, bytes_accessed=0, transcendentals=0),
    )(place, *operands)


def paired(ring):
    return lambda i: ring[0] + i * (ring[1] - ring[0])


def reduce_scatter(place, table, sign, grad, index, hmat, staged):
    code = functools.partial(encode, place, table, sign, grad, index, hmat)
    pair = ((2, BLOCK, WIDTH), jnp.bfloat16)
    both = pl.BlockSpec((None, PART, WIDTH), lambda i, j, place_ref: (i, j, 0))
    grid = (2, BLOCK // PART)

    def round_of(*plan):
        jobs = [(near, paired(ring), [(v, both) for v in arrived], both, *pair) for _, near, ring, arrived in plan]
        codes = code(grid, jobs)
        return [hop(v, "first", step) for v, (step, *_) in zip(codes, plan, strict=True)]

    up_far, down_far = round_of((1, 2, RING0, ()), (-1, 2, RING1, ()))
    up_own, down_own = round_of((1, 1, RING1, ()), (-1, 3, RING0, ()))
    single = pl.BlockSpec((PART, WIDTH), lambda i, j, place_ref: (j, 0))
    low = ((BLOCK, WIDTH), jnp.bfloat16)

    def of_slot(slot):
        return pl.BlockSpec((None, PART, WIDTH), lambda i, j, place_ref: (slot, j, 0))

    def sums_of(slot):
        plan = ((1, 1, RING0[slot], up_far), (-1, 3, RING1[slot], down_far))
        jobs = [(near, lambda i, far=far: far, [(v, of_slot(slot))], single, *low) for _, near, far, v in plan]
        return [hop(v, "first", step) for v, (step, *_) in zip(code((1, BLOCK // PART), jobs, staged), plan, strict=True)]

    def own_of(slot, *rings):
        plan, jobs = [], []
        for ring, whole in rings:
            far, part = (RING0[slot], down_own) if ring == 0 else (RING1[slot], up_own)
            shape = low if far else ((BLOCK, WIDTH), jnp.float32)
            jobs.append((0, lambda i, far=far: far, [(whole, single), (part, of_slot(slot))], single, *shape))
            plan.append(far)
        values = code((1, BLOCK // PART), jobs)
        return [in_vmem(hop(v, "second", far)) if far else v for v, far in zip(values, plan, strict=True)]

    early_up, early_down = sums_of(0)
    late_up, late_down = sums_of(1)
    two, three = own_of(0, (0, early_up), (1, early_down))
    (one,) = own_of(1, (0, late_up))
    (own,) = own_of(1, (1, late_down))
    return [own, two, one, three]


def decode_kernel(place_ref, table_ref, sign_ref, hmat_ref, own_ref, two_ref, one_ref, three_ref, index_ref, plain_ref, square_ref, sum_ref):
    f32 = jnp.float32

    @pl.when(pl.program_id(0) == 0)
    def _():
        sum_ref[...] = jnp.zeros_like(sum_ref)

    scales = row_scales([index_ref], table_ref, False) * (1.0 / math.sqrt(TILE))
    sign = (2 * sign_ref[...] - 1).reshape(1, WIDTH).astype(f32)
    square = sum_ref[...]
    for tile in range(TILES):
        cols = slice(tile * TILE, (tile + 1) * TILE)
        value = own_ref[:, cols] + two_ref[:, cols].astype(f32) + one_ref[:, cols].astype(f32) + three_ref[:, cols].astype(f32)
        plain = jnp.zeros(value.shape, f32)
        for _ in range(3):
            piece = value.astype(jnp.bfloat16)
            plain = plain + jnp.dot(piece, hmat_ref[...], preferred_element_type=f32)
            value = value - piece.astype(f32)
        plain = plain * scales[:, tile : tile + 1] * sign[:, cols]
        plain_ref[:, cols] = plain
        parts = jnp.sum((plain * plain).reshape(-1, 8, TILE), axis=0)
        square = square + parts[:, :128] + parts[:, 128:]
    sum_ref[...] = square
    square_ref[...] = jnp.broadcast_to(jnp.sum(square, axis=0, keepdims=True), square_ref.shape)


def decode(place, table, sign, terms, index, hmat, copies):
    parts = BLOCK // PART
    single = pl.BlockSpec((PART, WIDTH), lambda j, place_ref: (j, 0))
    return pl.pallas_call(
        decode_kernel,
        out_shape=(
            pltpu.VMEM((BLOCK, WIDTH), jnp.float32),
            pltpu.HBM((copies, 128), jnp.float32),
        ),
        grid_spec=pltpu.PrefetchScalarGridSpec(
            num_scalar_prefetch=1,
            grid=(parts,),
            in_specs=[
                pl.BlockSpec(memory_space=pltpu.SMEM),
                pl.BlockSpec((WIDTH,), lambda j, place_ref: (0,)),
                pl.BlockSpec((TILE, TILE), lambda j, place_ref: (0, 0)),
                *[single] * 4,
                pl.BlockSpec((TILES, PART), lambda j, place_ref: (0, block_at(place_ref, 0, 0) * parts + j)),
            ],
            out_specs=(
                single,
                pl.BlockSpec((copies, 128), lambda j, place_ref: (0, 0)),
            ),
            scratch_shapes=[pltpu.VMEM((8, 128), jnp.float32)],
        ),
        compiler_params=pltpu.CompilerParams(vmem_limit_bytes=VMEM_BYTES),
        cost_estimate=pl.CostEstimate(flops=0, bytes_accessed=0, transcendentals=0),
    )(place, table, sign, hmat, *terms, index)


MEAN_SCALE = 0.02 / (1.0 - 0.9**10)
VAR_SCALE = 1.0 / (1.0 - 0.95**10)


def clip_factor(square_ref):
    square = jnp.sum(jnp.sum(square_ref[...], axis=0, keepdims=True), axis=1, keepdims=True)
    return LIMIT / jnp.maximum(jnp.sqrt(square), LIMIT)


def stepped(master, new_mean, new_var):
    spread = new_var * VAR_SCALE
    spread = spread * lax.rsqrt(spread)
    return 0.998 * master - new_mean * MEAN_SCALE / (spread + 1e-08)


def weights_kernel(square_ref, plain_ref, master_ref, mean_ref, var_ref, out_ref):
    grad = plain_ref[...] * clip_factor(square_ref)
    new_mean = 0.9 * mean_ref[...] + 0.1 * grad
    new_var = 0.95 * var_ref[...] + 0.05 * grad * grad
    out_ref[...] = stepped(master_ref[...], new_mean, new_var).astype(jnp.bfloat16)


def state_kernel(square_ref, plain_ref, master_ref, mean_ref, var_ref, new_master_ref, new_mean_ref, new_var_ref):
    grad = plain_ref[...] * clip_factor(square_ref)
    new_mean = 0.9 * mean_ref[...] + 0.1 * grad
    new_var = 0.95 * var_ref[...] + 0.05 * grad * grad
    new_mean_ref[...] = new_mean
    new_var_ref[...] = new_var
    new_master_ref[...] = stepped(master_ref[...], new_mean, new_var)


def adamw(kernel, out_shape, square, plain, master, mean, var):
    rows = pl.BlockSpec((STEP, WIDTH), lambda j: (j, 0))
    return pl.pallas_call(
        kernel,
        out_shape=out_shape,
        grid=(BLOCK // STEP,),
        in_specs=[pl.BlockSpec(square.shape, lambda j: (0, 0))] + [rows] * 4,
        out_specs=jax.tree.map(lambda _: rows, out_shape),
        compiler_params=pltpu.CompilerParams(vmem_limit_bytes=VMEM_BYTES),
        cost_estimate=pl.CostEstimate(flops=0, bytes_accessed=0, transcendentals=0),
    )(square, plain, master, mean, var)


def stage_kernel(*refs):
    for source, target in zip(refs[:3], refs[3:6], strict=True):
        target[...] = source[...]
    refs[6][...] = jnp.zeros_like(refs[6])


def stage(*state):
    rows = pl.BlockSpec((STEP, WIDTH), lambda j: (j, 0))
    return pl.pallas_call(
        stage_kernel,
        out_shape=[pltpu.VMEM(v.shape, v.dtype) for v in state] + [jax.ShapeDtypeStruct((8, 128), jnp.float32)],
        grid=(BLOCK // STEP,),
        in_specs=[rows] * 3,
        out_specs=[rows] * 3 + [pl.BlockSpec((8, 128), lambda j: (0, 0))],
        compiler_params=pltpu.CompilerParams(vmem_limit_bytes=VMEM_BYTES),
        cost_estimate=pl.CostEstimate(flops=0, bytes_accessed=0, transcendentals=0),
    )(*state)


def after(value, first):
    anywhere = pl.BlockSpec(memory_space=pl.ANY)
    return pl.pallas_call(
        lambda *_: None,
        out_shape=jax.ShapeDtypeStruct(value.shape, value.dtype),
        in_specs=[anywhere, anywhere],
        out_specs=anywhere,
        input_output_aliases={0: 0},
        compiler_params=pltpu.CompilerParams(vmem_limit_bytes=VMEM_BYTES),
    )(value, first)


def fill_kernel(places, at_ref, *refs):
    count = len(places)
    out_ref, tile_ref, sems = refs[-3:]
    tile_ref[...] = jnp.zeros_like(tile_ref)
    chip, core = at_ref[0] // 2, at_ref[0] % 2
    copies = []
    for j, (step, swapped, row) in enumerate(places):
        source = (chip + SIDE - step + 2 * step * core) % SIDE
        column = pl.multiple_of((source * 2 + (1 - core if swapped else core)) * WIDTH, WIDTH)
        target = out_ref.at[pl.ds(row, refs[j].shape[0]), pl.ds(column, WIDTH)]
        copies.append(pltpu.make_async_copy(refs[j], target, sems.at[j]))
    for copy in copies:
        copy.start()
    for copy in copies:
        copy.wait()


def fill(at, places, blocks, weights=None):
    anywhere = pl.BlockSpec(memory_space=pl.ANY)
    given = [] if weights is None else [weights]
    return pl.pallas_call(
        functools.partial(fill_kernel, places),
        out_shape=(pltpu.HBM((BLOCK, D), jnp.bfloat16), jax.ShapeDtypeStruct((8, 128), jnp.float32)),
        in_specs=[pl.BlockSpec(memory_space=pltpu.SMEM)] + [pl.BlockSpec(v.shape, lambda: (0, 0)) for v in blocks] + [anywhere] * len(given),
        out_specs=(anywhere, pl.BlockSpec((8, 128), lambda: (0, 0))),
        scratch_shapes=[pltpu.SemaphoreType.DMA((len(blocks),))],
        input_output_aliases={len(blocks) + 1: 0} if given else {},
        compiler_params=pltpu.CompilerParams(vmem_limit_bytes=VMEM_BYTES),
        cost_estimate=pl.CostEstimate(flops=0, bytes_accessed=0, transcendentals=0),
    )(at, *blocks, *given)


def along_y(value):
    pairs = [(y * 2 + core, (y + 1 - 2 * core) % SIDE * 2 + core) for y in range(SIDE) for core in range(2)]
    return lax.ppermute(value, "fsdp", pairs)


def to_other_core(value):
    return lax.ppermute(value, "fsdp", [(i, i ^ 1) for i in range(8)])


def gather(low, state):
    at = lax.axis_index("fsdp").reshape(1)
    one = along_y(low)
    other = to_other_core(low)
    one_other = along_y(other)
    one = after(one, state)
    two = along_y(one)
    one_swapped = to_other_core(one)
    halves = [to_other_core(one_other[row : row + PART]) for row in (0, PART)]
    near = ((0, False, 0), (0, True, 0), (1, False, 0), (1, True, 0), (-1, True, 0), (-1, False, 0), (-1, False, PART))
    weights, filled = fill(at, near, (low, other, one, one_other, one_swapped, *halves))
    two = after(two, filled)
    two_swapped = to_other_core(two)
    return fill(at, ((2, False, 0), (2, True, 0)), (two, two_swapped), weights)[0]


def on_device(grad_shards, hadamard_signs, scale_index, scale_table, master, mean_moment, var_moment):
    grad, scale_index, master, mean_moment, var_moment = map(in_hbm, (grad_shards[0], scale_index, master, mean_moment, var_moment))
    scale_table = in_hbm(scale_table)
    place = (lax.axis_index("dp") * 2 + (lax.axis_index("fsdp") & 1)).reshape(1)
    sign = in_hbm(hadamard_signs)
    hmat = in_hbm(jnp.asarray(hadamard(TILE)))
    *state, staged = stage(master, mean_moment, var_moment)
    terms = reduce_scatter(place, scale_table, sign, grad, scale_index, hmat, staged)
    plain, square = decode(place, scale_table, sign, terms, scale_index, hmat, lax.axis_size(("dp", "fsdp")))
    square = lax.all_to_all(square, ("dp", "fsdp"), 0, 0, tiled=True)
    state = [in_vmem(v) for v in (plain, *state)]
    low = adamw(weights_kernel, jax.ShapeDtypeStruct((BLOCK, WIDTH), jnp.bfloat16), square, *state)
    new_state = adamw(state_kernel, (jax.ShapeDtypeStruct(master.shape, jnp.float32),) * 3, square, *state)
    return *new_state, gather(low, in_hbm(new_state[0]))


def solution(mesh):
    return jax.shard_map(
        on_device,
        mesh=mesh,
        in_specs=(
            P("dp", None, "fsdp"),
            P("fsdp"),
            P("fsdp", None),
            P(),
            P("dp", "fsdp"),
            P("dp", "fsdp"),
            P("dp", "fsdp"),
        ),
        out_specs=(P("dp", "fsdp"), P("dp", "fsdp"), P("dp", "fsdp"), P("dp", None)),
        check_vma=False,
    )
```

```python
import functools
import math

import jax
import jax.numpy as jnp
import ml_dtypes
import numpy as np
from jax import lax
from jax.experimental import pallas as pl
from jax.experimental.pallas import tpu as pltpu
from jax.sharding import PartitionSpec as P

D = 6144
ROWS = 8192
TILE = 256
WIDTH = 768
TILES = WIDTH // TILE
SIDE = 4
BLOCK = 512
PART = 256
STEP = 128
CUTS = 4
RING0, RING1 = (2, 1), (3, 0)
LIMIT = 4.0 * math.sqrt(ROWS * D)
VMEM_BYTES = 14 * 1024 * 1024


def hadamard(length):
    index = np.arange(length)
    common_bits = index[:, None] & index[None, :]
    parity = np.zeros((length, length), np.int32)
    for bit_pos in range(length.bit_length() - 1):
        parity = parity ^ common_bits >> bit_pos & 1
    return (1 - 2 * parity).astype(ml_dtypes.bfloat16)


def hop(value, axis, step):
    pairs = []
    for device in range(128):
        x, z, core = device // 32, device // 8 % SIDE, device % 2
        if (axis == "first") == (core == 0):
            x = (x + step) % SIDE
        else:
            z = (z + step) % SIDE
        pairs.append((device, (x * SIDE + z) * 8 + device % 8))
    return lax.ppermute(value, ("dp", "fsdp"), pairs)


def in_hbm(value):
    return pltpu.with_memory_space_constraint(value, pltpu.HBM)


def in_vmem(value):
    return pltpu.with_memory_space_constraint(value, pltpu.VMEM)


def row_scales(index_refs, table_ref, inverse):
    index = jnp.concatenate([ref[...] for ref in index_refs], axis=1)
    scale = jnp.zeros(index.shape, jnp.float32)
    for level in range(table_ref.shape[0]):
        scale = jnp.where(index == level, table_ref[level], scale)
    if inverse:
        scale = 1.0 / (math.sqrt(TILE) * scale)
    ones = jnp.ones((8 - index.shape[0], index.shape[1]), jnp.float32)
    return jnp.concatenate([scale, ones], axis=0).T


def encode_kernel(counts, ordered, place_ref, table_ref, sign_ref, hmat_ref, *refs):
    jobs = len(counts)
    inputs, out_refs = iter(refs[int(ordered) : -jobs]), refs[-jobs:]
    grad_refs, index_refs, arrived_refs = [], [], []
    for count in counts:
        grad_refs.append(next(inputs))
        index_refs.append(next(inputs))
        arrived_refs.append([next(inputs) for _ in range(count)])
    steps = row_scales(index_refs, table_ref, True)
    sign = (2 * sign_ref[...] - 1).reshape(1, WIDTH).astype(jnp.bfloat16)
    for tile in range(TILES):
        cols = slice(tile * TILE, (tile + 1) * TILE)
        signed = jnp.concatenate([ref[:, cols] for ref in grad_refs], axis=0) * sign[:, cols]
        rotated = jnp.dot(signed, hmat_ref[...], preferred_element_type=jnp.float32)
        codes = jnp.clip(rotated * steps[:, tile : tile + 1], -127.0, 127.0).astype(jnp.bfloat16)
        for job in range(jobs):
            code = codes[job * PART : (job + 1) * PART]
            if arrived_refs[job]:
                total = code.astype(jnp.float32)
                for ref in arrived_refs[job]:
                    total = total + ref[:, cols].astype(jnp.float32)
                code = total.astype(out_refs[job].dtype)
            out_refs[job][:, cols] = code


def block_at(place_ref, near, far):
    place = place_ref[0]
    x, z, core = place // (2 * SIDE), place // 2 % SIDE, place % 2
    x, z = x + jnp.where(core == 0, near, far), z + jnp.where(core == 0, far, near)
    return lax.rem(x, SIDE) * SIDE + lax.rem(z, SIDE)


def encode(place, table, sign, grad, index, hmat, grid, jobs, after=None):
    in_specs = [
        pl.BlockSpec(memory_space=pltpu.SMEM),
        pl.BlockSpec((WIDTH,), lambda *_: (0,)),
        pl.BlockSpec((TILE, TILE), lambda *_: (0, 0)),
    ]
    operands, out_specs, out_shape = [table, sign, hmat], [], []
    if after is not None:
        in_specs.append(pl.BlockSpec((8, 128), lambda *_: (0, 0)))
        operands.append(after)
    parts = BLOCK // PART
    for near, far, arrived, spec, shape, dtype in jobs:
        rows = functools.partial(lambda near, far, i, j, place_ref: block_at(place_ref, near, far(i)) * parts + j, near, far)
        in_specs.append(pl.BlockSpec((PART, WIDTH), functools.partial(lambda rows, *at: (rows(*at), 0), rows)))
        in_specs.append(pl.BlockSpec((TILES, PART), functools.partial(lambda rows, *at: (0, rows(*at)), rows)))
        operands += [grad, index]
        for value, its_spec in arrived:
            in_specs.append(its_spec)
            operands.append(value)
        out_specs.append(spec)
        out_shape.append(jax.ShapeDtypeStruct(shape, dtype))
    blocks = len(jobs) * grid[0] * parts
    return pl.pallas_call(
        functools.partial(encode_kernel, [len(job[2]) for job in jobs], after is not None),
        out_shape=out_shape,
        grid_spec=pltpu.PrefetchScalarGridSpec(num_scalar_prefetch=1, grid=grid, in_specs=in_specs, out_specs=out_specs),
        compiler_params=pltpu.CompilerParams(vmem_limit_bytes=VMEM_BYTES),
        cost_estimate=pl.CostEstimate(flops=0, bytes_accessed=0, transcendentals=0),
    )(place, *operands)


def paired(ring):
    return lambda i: ring[0] + i * (ring[1] - ring[0])


def reduce_scatter(place, table, sign, grad, index, hmat, staged):
    code = functools.partial(encode, place, table, sign, grad, index, hmat)
    pair = ((2, BLOCK, WIDTH), jnp.bfloat16)
    both = pl.BlockSpec((None, PART, WIDTH), lambda i, j, place_ref: (i, j, 0))
    grid = (2, BLOCK // PART)

    def round_of(*plan):
        jobs = [(near, paired(ring), [(v, both) for v in arrived], both, *pair) for _, near, ring, arrived in plan]
        codes = code(grid, jobs)
        return [hop(v, "first", step) for v, (step, *_) in zip(codes, plan, strict=True)]

    up_far, down_far = round_of((1, 2, RING0, ()), (-1, 2, RING1, ()))
    up_own, down_own = round_of((1, 1, RING1, ()), (-1, 3, RING0, ()))
    single = pl.BlockSpec((PART, WIDTH), lambda i, j, place_ref: (j, 0))
    low = ((BLOCK, WIDTH), jnp.bfloat16)

    def of_slot(slot):
        return pl.BlockSpec((None, PART, WIDTH), lambda i, j, place_ref: (slot, j, 0))

    def sums_of(slot):
        plan = ((1, 1, RING0[slot], up_far), (-1, 3, RING1[slot], down_far))
        jobs = [(near, lambda i, far=far: far, [(v, of_slot(slot))], single, *low) for _, near, far, v in plan]
        return [hop(v, "first", step) for v, (step, *_) in zip(code((1, BLOCK // PART), jobs, staged), plan, strict=True)]

    def own_of(slot, *rings):
        plan, jobs = [], []
        for ring, whole in rings:
            far, part = (RING0[slot], down_own) if ring == 0 else (RING1[slot], up_own)
            shape = low if far else ((BLOCK, WIDTH), jnp.float32)
            jobs.append((0, lambda i, far=far: far, [(whole, single), (part, of_slot(slot))], single, *shape))
            plan.append(far)
        values = code((1, BLOCK // PART), jobs)
        return [in_vmem(hop(v, "second", far)) if far else v for v, far in zip(values, plan, strict=True)]

    early_up, early_down = sums_of(0)
    late_up, late_down = sums_of(1)
    two, three = own_of(0, (0, early_up), (1, early_down))
    (one,) = own_of(1, (0, late_up))
    (own,) = own_of(1, (1, late_down))
    return [own, two, one, three]


def decode_kernel(place_ref, table_ref, sign_ref, hmat_ref, own_ref, two_ref, one_ref, three_ref, index_ref, plain_ref, square_ref, sum_ref):
    f32 = jnp.float32

    @pl.when(pl.program_id(0) == 0)
    def _():
        sum_ref[...] = jnp.zeros_like(sum_ref)

    scales = row_scales([index_ref], table_ref, False) * (1.0 / math.sqrt(TILE))
    sign = (2 * sign_ref[...] - 1).reshape(1, WIDTH).astype(f32)
    square = sum_ref[...]
    for tile in range(TILES):
        cols = slice(tile * TILE, (tile + 1) * TILE)
        value = own_ref[:, cols] + two_ref[:, cols].astype(f32) + one_ref[:, cols].astype(f32) + three_ref[:, cols].astype(f32)
        plain = jnp.zeros(value.shape, f32)
        for _ in range(3):
            piece = value.astype(jnp.bfloat16)
            plain = plain + jnp.dot(piece, hmat_ref[...], preferred_element_type=f32)
            value = value - piece.astype(f32)
        plain = plain * scales[:, tile : tile + 1] * sign[:, cols]
        plain_ref[:, cols] = plain
        parts = jnp.sum((plain * plain).reshape(-1, 8, TILE), axis=0)
        square = square + parts[:, :128] + parts[:, 128:]
    sum_ref[...] = square
    square_ref[...] = jnp.broadcast_to(jnp.sum(square, axis=0, keepdims=True), square_ref.shape)


def decode(place, table, sign, terms, index, hmat, copies):
    parts = BLOCK // BLOCK
    single = pl.BlockSpec((BLOCK, WIDTH), lambda j, place_ref: (j, 0))
    return pl.pallas_call(
        decode_kernel,
        out_shape=(
            pltpu.VMEM((BLOCK, WIDTH), jnp.float32),
            pltpu.HBM((copies, 128), jnp.float32),
        ),
        grid_spec=pltpu.PrefetchScalarGridSpec(
            num_scalar_prefetch=1,
            grid=(parts,),
            in_specs=[
                pl.BlockSpec(memory_space=pltpu.SMEM),
                pl.BlockSpec((WIDTH,), lambda j, place_ref: (0,)),
                pl.BlockSpec((TILE, TILE), lambda j, place_ref: (0, 0)),
                *[single] * 4,
                pl.BlockSpec((TILES, BLOCK), lambda j, place_ref: (0, block_at(place_ref, 0, 0) * parts + j)),
            ],
            out_specs=(
                single,
                pl.BlockSpec((copies, 128), lambda j, place_ref: (0, 0)),
            ),
            scratch_shapes=[pltpu.VMEM((8, 128), jnp.float32)],
        ),
        compiler_params=pltpu.CompilerParams(vmem_limit_bytes=VMEM_BYTES),
        cost_estimate=pl.CostEstimate(flops=0, bytes_accessed=0, transcendentals=0),
    )(place, table, sign, hmat, *terms, index)


MEAN_SCALE = 0.02 / (1.0 - 0.9**10)
VAR_SCALE = 1.0 / (1.0 - 0.95**10)


def clip_factor(square_ref):
    square = jnp.sum(jnp.sum(square_ref[...], axis=0, keepdims=True), axis=1, keepdims=True)
    return LIMIT / jnp.maximum(jnp.sqrt(square), LIMIT)


def stepped(master, new_mean, new_var):
    spread = new_var * VAR_SCALE
    spread = spread * lax.rsqrt(spread)
    return 0.998 * master - new_mean * MEAN_SCALE / (spread + 1e-08)


def weights_kernel(square_ref, plain_ref, master_ref, mean_ref, var_ref, out_ref):
    grad = plain_ref[...] * clip_factor(square_ref)
    new_mean = 0.9 * mean_ref[...] + 0.1 * grad
    new_var = 0.95 * var_ref[...] + 0.05 * grad * grad
    out_ref[...] = stepped(master_ref[...], new_mean, new_var).astype(jnp.bfloat16)


def state_kernel(square_ref, plain_ref, master_ref, mean_ref, var_ref, new_master_ref, new_mean_ref, new_var_ref):
    grad = plain_ref[...] * clip_factor(square_ref)
    new_mean = 0.9 * mean_ref[...] + 0.1 * grad
    new_var = 0.95 * var_ref[...] + 0.05 * grad * grad
    new_mean_ref[...] = new_mean
    new_var_ref[...] = new_var
    new_master_ref[...] = stepped(master_ref[...], new_mean, new_var)


def adamw(kernel, out_shape, square, plain, master, mean, var):
    rows = pl.BlockSpec((STEP, WIDTH), lambda j: (j, 0))
    return pl.pallas_call(
        kernel,
        out_shape=out_shape,
        grid=(BLOCK // STEP,),
        in_specs=[pl.BlockSpec(square.shape, lambda j: (0, 0))] + [rows] * 4,
        out_specs=jax.tree.map(lambda _: rows, out_shape),
        compiler_params=pltpu.CompilerParams(vmem_limit_bytes=VMEM_BYTES),
        cost_estimate=pl.CostEstimate(flops=0, bytes_accessed=0, transcendentals=0),
    )(square, plain, master, mean, var)


def stage_kernel(*refs):
    for source, target in zip(refs[:3], refs[3:6], strict=True):
        target[...] = source[...]
    refs[6][...] = jnp.zeros_like(refs[6])


def stage(*state):
    rows = pl.BlockSpec((STEP, WIDTH), lambda j: (j, 0))
    return pl.pallas_call(
        stage_kernel,
        out_shape=[pltpu.VMEM(v.shape, v.dtype) for v in state] + [jax.ShapeDtypeStruct((8, 128), jnp.float32)],
        grid=(BLOCK // STEP,),
        in_specs=[rows] * 3,
        out_specs=[rows] * 3 + [pl.BlockSpec((8, 128), lambda j: (0, 0))],
        compiler_params=pltpu.CompilerParams(vmem_limit_bytes=VMEM_BYTES),
        cost_estimate=pl.CostEstimate(flops=0, bytes_accessed=0, transcendentals=0),
    )(*state)


def after(value, first):
    anywhere = pl.BlockSpec(memory_space=pl.ANY)
    return pl.pallas_call(
        lambda *_: None,
        out_shape=jax.ShapeDtypeStruct(value.shape, value.dtype),
        in_specs=[anywhere, anywhere],
        out_specs=anywhere,
        input_output_aliases={0: 0},
        compiler_params=pltpu.CompilerParams(vmem_limit_bytes=VMEM_BYTES),
    )(value, first)


def fill_kernel(places, out_at, *refs):
    out_ref, sems = refs[out_at], refs[-1]
    for tile_ref in refs[out_at + 1 : -1]:
        tile_ref[...] = jnp.zeros_like(tile_ref)
    at = lax.axis_index("fsdp")
    chip, core = at // 2, at % 2
    copies = []
    for j, (step, swapped, row) in enumerate(places):
        sender = (chip + SIDE - step + 2 * step * core) % SIDE
        column = pl.multiple_of((sender * 2 + (1 - core if swapped else core)) * WIDTH, WIDTH)
        height = refs[j].shape[0] // CUTS
        for cut in range(CUTS):
            source = refs[j].at[pl.ds(cut * height, height), :]
            target = out_ref.at[pl.ds(row + cut * height, height), pl.ds(column, WIDTH)]
            copies.append(pltpu.make_async_copy(source, target, sems.at[len(copies)]))
    for copy in copies:
        copy.start()
    for copy in copies:
        copy.wait()


def fill(places, blocks, weights=None, tile=False):
    anywhere = pl.BlockSpec(memory_space=pl.ANY)
    given = [] if weights is None else [weights]
    return pl.pallas_call(
        functools.partial(fill_kernel, places, len(blocks) + len(given)),
        out_shape=[pltpu.HBM((BLOCK, D), jnp.bfloat16)] + [jax.ShapeDtypeStruct((8, 128), jnp.float32)] * tile,
        in_specs=[anywhere] * len(blocks) + [anywhere] * len(given),
        out_specs=[anywhere] + [pl.BlockSpec((8, 128), lambda: (0, 0))] * tile,
        scratch_shapes=[pltpu.SemaphoreType.DMA((CUTS * len(blocks),))],
        input_output_aliases={len(blocks): 0} if given else {},
        compiler_params=pltpu.CompilerParams(vmem_limit_bytes=VMEM_BYTES),
        cost_estimate=pl.CostEstimate(flops=0, bytes_accessed=0, transcendentals=0),
    )(*map(in_vmem, blocks), *given)


def along_y(value):
    pairs = [(y * 2 + core, (y + 1 - 2 * core) % SIDE * 2 + core) for y in range(SIDE) for core in range(2)]
    return lax.ppermute(value, "fsdp", pairs)


def to_other_core(value):
    return lax.ppermute(value, "fsdp", [(i, i ^ 1) for i in range(8)])


def gather(low, state):
    one = along_y(low)
    other = to_other_core(low)
    one_other = along_y(other)
    one = after(one, state)
    two = along_y(one)
    one_swapped = to_other_core(one)
    halves = [to_other_core(one_other[row : row + PART]) for row in (0, PART)]
    near = ((0, False, 0), (0, True, 0), (1, False, 0), (1, True, 0), (-1, True, 0), (-1, False, 0), (-1, False, PART))
    weights, filled = fill(near, (low, other, one, one_other, one_swapped, *halves), tile=True)
    two = after(two, filled)
    two_swapped = to_other_core(two)
    weights = fill(((2, False, 0),), (two,), weights)[0]
    return fill(((2, True, 0),), (two_swapped,), weights)[0]


def on_device(grad_shards, hadamard_signs, scale_index, scale_table, master, mean_moment, var_moment):
    grad, scale_index, master, mean_moment, var_moment = map(in_hbm, (grad_shards[0], scale_index, master, mean_moment, var_moment))
    scale_table = in_hbm(scale_table)
    place = (lax.axis_index("dp") * 2 + (lax.axis_index("fsdp") & 1)).reshape(1)
    sign = in_hbm(hadamard_signs)
    hmat = in_hbm(jnp.asarray(hadamard(TILE)))
    *state, staged = stage(master, mean_moment, var_moment)
    terms = reduce_scatter(place, scale_table, sign, grad, scale_index, hmat, staged)
    plain, square = decode(place, scale_table, sign, terms, scale_index, hmat, lax.axis_size(("dp", "fsdp")))
    square = lax.all_to_all(square, ("dp", "fsdp"), 0, 0, tiled=True)
    state = [in_vmem(v) for v in (plain, *state)]
    low = adamw(weights_kernel, jax.ShapeDtypeStruct((BLOCK, WIDTH), jnp.bfloat16), square, *state)
    new_state = adamw(state_kernel, (jax.ShapeDtypeStruct(master.shape, jnp.float32),) * 3, square, *state)
    return *new_state, gather(low, in_hbm(new_state[0]))


def solution(mesh):
    return jax.shard_map(
        on_device,
        mesh=mesh,
        in_specs=(
            P("dp", None, "fsdp"),
            P("fsdp"),
            P("fsdp", None),
            P(),
            P("dp", "fsdp"),
            P("dp", "fsdp"),
            P("dp", "fsdp"),
        ),
        out_specs=(P("dp", "fsdp"), P("dp", "fsdp"), P("dp", "fsdp"), P("dp", None)),
        check_vma=False,
    )
```

```python
import functools
import math

import jax
import jax.numpy as jnp
import ml_dtypes
import numpy as np
from jax import lax
from jax.experimental import pallas as pl
from jax.experimental.pallas import tpu as pltpu
from jax.sharding import PartitionSpec as P

D = 6144
ROWS = 8192
TILE = 256
WIDTH = 768
TILES = WIDTH // TILE
SIDE = 4
BLOCK = 512
PART = 256
STEP = 128
CUTS = 4
RING0, RING1 = (2, 1), (3, 0)
LIMIT = 4.0 * math.sqrt(ROWS * D)
VMEM_BYTES = 14 * 1024 * 1024


def hadamard(length):
    index = np.arange(length)
    common_bits = index[:, None] & index[None, :]
    parity = np.zeros((length, length), np.int32)
    for bit_pos in range(length.bit_length() - 1):
        parity = parity ^ common_bits >> bit_pos & 1
    return (1 - 2 * parity).astype(ml_dtypes.bfloat16)


def hop(value, axis, step):
    pairs = []
    for device in range(128):
        x, z, core = device // 32, device // 8 % SIDE, device % 2
        if (axis == "first") == (core == 0):
            x = (x + step) % SIDE
        else:
            z = (z + step) % SIDE
        pairs.append((device, (x * SIDE + z) * 8 + device % 8))
    return lax.ppermute(value, ("dp", "fsdp"), pairs)


def in_hbm(value):
    return pltpu.with_memory_space_constraint(value, pltpu.HBM)


def in_vmem(value):
    return pltpu.with_memory_space_constraint(value, pltpu.VMEM)


def row_scales(index_refs, table_ref, inverse):
    index = jnp.concatenate([ref[...] for ref in index_refs], axis=1)
    scale = jnp.zeros(index.shape, jnp.float32)
    for level in range(table_ref.shape[0]):
        scale = jnp.where(index == level, table_ref[level], scale)
    if inverse:
        scale = 1.0 / (math.sqrt(TILE) * scale)
    ones = jnp.ones((8 - index.shape[0], index.shape[1]), jnp.float32)
    return jnp.concatenate([scale, ones], axis=0).T


def encode_kernel(counts, targets, ordered, place_ref, table_ref, sign_ref, hmat_ref, *refs):
    jobs = len(counts)
    outs = max(out for out, _ in targets) + 1
    inputs, outs = iter(refs[int(ordered) : -outs]), refs[-outs:]
    out_refs = [outs[out] if slot is None else outs[out].at[slot] for out, slot in targets]
    grad_refs, index_refs, arrived_refs = [], [], []
    for count in counts:
        grad_refs.append(next(inputs))
        index_refs.append(next(inputs))
        arrived_refs.append([next(inputs) for _ in range(count)])
    steps = row_scales(index_refs, table_ref, True)
    sign = (2 * sign_ref[...] - 1).reshape(1, WIDTH).astype(jnp.bfloat16)
    for tile in range(TILES):
        cols = slice(tile * TILE, (tile + 1) * TILE)
        signed = jnp.concatenate([ref[:, cols] for ref in grad_refs], axis=0) * sign[:, cols]
        rotated = jnp.dot(signed, hmat_ref[...], preferred_element_type=jnp.float32)
        codes = jnp.clip(rotated * steps[:, tile : tile + 1], -127.0, 127.0).astype(jnp.bfloat16)
        for job in range(jobs):
            code = codes[job * PART : (job + 1) * PART]
            if arrived_refs[job]:
                total = code.astype(jnp.float32)
                for ref in arrived_refs[job]:
                    total = total + ref[:, cols].astype(jnp.float32)
                code = total.astype(out_refs[job].dtype)
            out_refs[job][:, cols] = code


def block_at(place_ref, near, far):
    place = place_ref[0]
    x, z, core = place // (2 * SIDE), place // 2 % SIDE, place % 2
    x, z = x + jnp.where(core == 0, near, far), z + jnp.where(core == 0, far, near)
    return lax.rem(x, SIDE) * SIDE + lax.rem(z, SIDE)


def encode(place, table, sign, grad, index, hmat, grid, jobs, after=None):
    in_specs = [
        pl.BlockSpec(memory_space=pltpu.SMEM),
        pl.BlockSpec((WIDTH,), lambda *_: (0,)),
        pl.BlockSpec((TILE, TILE), lambda *_: (0, 0)),
    ]
    operands, out_specs, out_shape = [table, sign, hmat], [], []
    if after is not None:
        in_specs.append(pl.BlockSpec((8, 128), lambda *_: (0, 0)))
        operands.append(after)
    parts, targets = BLOCK // PART, []
    for near, far, arrived, spec, shape, dtype in jobs:
        rows = functools.partial(lambda near, far, i, j, place_ref: block_at(place_ref, near, far(i)) * parts + j, near, far)
        in_specs.append(pl.BlockSpec((PART, WIDTH), functools.partial(lambda rows, *at: (rows(*at), 0), rows)))
        in_specs.append(pl.BlockSpec((TILES, PART), functools.partial(lambda rows, *at: (0, rows(*at)), rows)))
        operands += [grad, index]
        for value, its_spec in arrived:
            in_specs.append(its_spec)
            operands.append(value)
        if spec is not None:
            out_specs.append(spec)
            out_shape.append(jax.ShapeDtypeStruct(shape, dtype))
        targets.append((len(out_specs) - 1, None if len(shape) == 2 else int(spec is None)))
    blocks = len(jobs) * grid[0] * parts
    return pl.pallas_call(
        functools.partial(encode_kernel, [len(job[2]) for job in jobs], targets, after is not None),
        out_shape=out_shape,
        grid_spec=pltpu.PrefetchScalarGridSpec(num_scalar_prefetch=1, grid=grid, in_specs=in_specs, out_specs=out_specs),
        compiler_params=pltpu.CompilerParams(vmem_limit_bytes=VMEM_BYTES),
        cost_estimate=pl.CostEstimate(flops=0, bytes_accessed=0, transcendentals=0),
    )(place, *operands)


def reduce_scatter(place, table, sign, grad, index, hmat, staged):
    code = functools.partial(encode, place, table, sign, grad, index, hmat)
    pair = ((2, BLOCK, WIDTH), jnp.bfloat16)
    both = pl.BlockSpec((2, PART, WIDTH), lambda i, j, place_ref: (0, j, 0))

    def round_of(*plan):
        jobs = []
        for _, near, ring in plan:
            jobs += [(near, lambda i, far=far: far, (), spec, *pair) for far, spec in zip(ring, (both, None), strict=True)]
        return [hop(v, "first", step) for v, (step, *_) in zip(code((1, BLOCK // PART), jobs), plan, strict=True)]

    up_far, down_far = round_of((1, 2, RING0), (-1, 2, RING1))
    up_own, down_own = round_of((1, 1, RING1), (-1, 3, RING0))
    single = pl.BlockSpec((PART, WIDTH), lambda i, j, place_ref: (j, 0))
    low = ((BLOCK, WIDTH), jnp.bfloat16)

    def of_slot(slot):
        return pl.BlockSpec((None, PART, WIDTH), lambda i, j, place_ref: (slot, j, 0))

    def sums_of(slot):
        plan = ((1, 1, RING0[slot], up_far), (-1, 3, RING1[slot], down_far))
        jobs = [(near, lambda i, far=far: far, [(v, of_slot(slot))], single, *low) for _, near, far, v in plan]
        return [hop(v, "first", step) for v, (step, *_) in zip(code((1, BLOCK // PART), jobs, staged), plan, strict=True)]

    def own_of(slot, *rings):
        plan, jobs = [], []
        for ring, whole in rings:
            far, part = (RING0[slot], down_own) if ring == 0 else (RING1[slot], up_own)
            shape = low if far else ((BLOCK, WIDTH), jnp.float32)
            jobs.append((0, lambda i, far=far: far, [(whole, single), (part, of_slot(slot))], single, *shape))
            plan.append(far)
        values = code((1, BLOCK // PART), jobs)
        return [in_vmem(hop(v, "second", far)) if far else v for v, far in zip(values, plan, strict=True)]

    early_up, early_down = sums_of(0)
    late_up, late_down = sums_of(1)
    two, three = own_of(0, (0, early_up), (1, early_down))
    (one,) = own_of(1, (0, late_up))
    (own,) = own_of(1, (1, late_down))
    return [own, two, one, three]


def decode_kernel(place_ref, table_ref, sign_ref, hmat_ref, own_ref, two_ref, one_ref, three_ref, index_ref, plain_ref, square_ref, sum_ref):
    f32 = jnp.float32

    @pl.when(pl.program_id(0) == 0)
    def _():
        sum_ref[...] = jnp.zeros_like(sum_ref)

    scales = row_scales([index_ref], table_ref, False) * (1.0 / math.sqrt(TILE))
    sign = (2 * sign_ref[...] - 1).reshape(1, WIDTH).astype(f32)
    square = sum_ref[...]
    for tile in range(TILES):
        cols = slice(tile * TILE, (tile + 1) * TILE)
        value = own_ref[:, cols] + two_ref[:, cols].astype(f32) + one_ref[:, cols].astype(f32) + three_ref[:, cols].astype(f32)
        plain = jnp.zeros(value.shape, f32)
        for _ in range(3):
            piece = value.astype(jnp.bfloat16)
            plain = plain + jnp.dot(piece, hmat_ref[...], preferred_element_type=f32)
            value = value - piece.astype(f32)
        plain = plain * scales[:, tile : tile + 1] * sign[:, cols]
        plain_ref[:, cols] = plain
        parts = jnp.sum((plain * plain).reshape(-1, 8, TILE), axis=0)
        square = square + parts[:, :128] + parts[:, 128:]
    sum_ref[...] = square
    square_ref[...] = jnp.broadcast_to(jnp.sum(square, axis=0, keepdims=True), square_ref.shape)


def decode(place, table, sign, terms, index, hmat, copies):
    parts = BLOCK // BLOCK
    single = pl.BlockSpec((BLOCK, WIDTH), lambda j, place_ref: (j, 0))
    return pl.pallas_call(
        decode_kernel,
        out_shape=(
            pltpu.VMEM((BLOCK, WIDTH), jnp.float32),
            pltpu.HBM((copies, 128), jnp.float32),
        ),
        grid_spec=pltpu.PrefetchScalarGridSpec(
            num_scalar_prefetch=1,
            grid=(parts,),
            in_specs=[
                pl.BlockSpec(memory_space=pltpu.SMEM),
                pl.BlockSpec((WIDTH,), lambda j, place_ref: (0,)),
                pl.BlockSpec((TILE, TILE), lambda j, place_ref: (0, 0)),
                *[single] * 4,
                pl.BlockSpec((TILES, BLOCK), lambda j, place_ref: (0, block_at(place_ref, 0, 0) * parts + j)),
            ],
            out_specs=(
                single,
                pl.BlockSpec((copies, 128), lambda j, place_ref: (0, 0)),
            ),
            scratch_shapes=[pltpu.VMEM((8, 128), jnp.float32)],
        ),
        compiler_params=pltpu.CompilerParams(vmem_limit_bytes=VMEM_BYTES),
        cost_estimate=pl.CostEstimate(flops=0, bytes_accessed=0, transcendentals=0),
    )(place, table, sign, hmat, *terms, index)


MEAN_SCALE = 0.02 / (1.0 - 0.9**10)
VAR_SCALE = 1.0 / (1.0 - 0.95**10)


def clip_factor(square_ref):
    square = jnp.sum(jnp.sum(square_ref[...], axis=0, keepdims=True), axis=1, keepdims=True)
    return LIMIT / jnp.maximum(jnp.sqrt(square), LIMIT)


def stepped(master, new_mean, new_var):
    spread = new_var * VAR_SCALE
    spread = spread * lax.rsqrt(spread)
    return 0.998 * master - new_mean * MEAN_SCALE / (spread + 1e-08)


def weights_kernel(square_ref, plain_ref, master_ref, mean_ref, var_ref, out_ref):
    grad = plain_ref[...] * clip_factor(square_ref)
    new_mean = 0.9 * mean_ref[...] + 0.1 * grad
    new_var = 0.95 * var_ref[...] + 0.05 * grad * grad
    out_ref[...] = stepped(master_ref[...], new_mean, new_var).astype(jnp.bfloat16)


def state_kernel(square_ref, plain_ref, master_ref, mean_ref, var_ref, new_master_ref, new_mean_ref, new_var_ref):
    grad = plain_ref[...] * clip_factor(square_ref)
    new_mean = 0.9 * mean_ref[...] + 0.1 * grad
    new_var = 0.95 * var_ref[...] + 0.05 * grad * grad
    new_mean_ref[...] = new_mean
    new_var_ref[...] = new_var
    new_master_ref[...] = stepped(master_ref[...], new_mean, new_var)


def adamw(kernel, out_shape, square, plain, master, mean, var):
    rows = pl.BlockSpec((STEP, WIDTH), lambda j: (j, 0))
    return pl.pallas_call(
        kernel,
        out_shape=out_shape,
        grid=(BLOCK // STEP,),
        in_specs=[pl.BlockSpec(square.shape, lambda j: (0, 0))] + [rows] * 4,
        out_specs=jax.tree.map(lambda _: rows, out_shape),
        compiler_params=pltpu.CompilerParams(vmem_limit_bytes=VMEM_BYTES),
        cost_estimate=pl.CostEstimate(flops=0, bytes_accessed=0, transcendentals=0),
    )(square, plain, master, mean, var)


def stage_kernel(*refs):
    for source, target in zip(refs[:3], refs[3:6], strict=True):
        target[...] = source[...]
    refs[6][...] = jnp.zeros_like(refs[6])


def stage(*state):
    rows = pl.BlockSpec((STEP, WIDTH), lambda j: (j, 0))
    return pl.pallas_call(
        stage_kernel,
        out_shape=[pltpu.VMEM(v.shape, v.dtype) for v in state] + [jax.ShapeDtypeStruct((8, 128), jnp.float32)],
        grid=(BLOCK // STEP,),
        in_specs=[rows] * 3,
        out_specs=[rows] * 3 + [pl.BlockSpec((8, 128), lambda j: (0, 0))],
        compiler_params=pltpu.CompilerParams(vmem_limit_bytes=VMEM_BYTES),
        cost_estimate=pl.CostEstimate(flops=0, bytes_accessed=0, transcendentals=0),
    )(*state)


def after(value, first):
    anywhere = pl.BlockSpec(memory_space=pl.ANY)
    return pl.pallas_call(
        lambda *_: None,
        out_shape=jax.ShapeDtypeStruct(value.shape, value.dtype),
        in_specs=[anywhere, anywhere],
        out_specs=anywhere,
        input_output_aliases={0: 0},
        compiler_params=pltpu.CompilerParams(vmem_limit_bytes=VMEM_BYTES),
    )(value, first)


def fill_kernel(places, out_at, *refs):
    out_ref, sems = refs[out_at], refs[-1]
    for tile_ref in refs[out_at + 1 : -1]:
        tile_ref[...] = jnp.zeros_like(tile_ref)
    at = lax.axis_index("fsdp")
    chip, core = at // 2, at % 2
    copies = []
    for j, (step, swapped, row) in enumerate(places):
        sender = (chip + SIDE - step + 2 * step * core) % SIDE
        column = pl.multiple_of((sender * 2 + (1 - core if swapped else core)) * WIDTH, WIDTH)
        height = refs[j].shape[0] // CUTS
        for cut in range(CUTS):
            source = refs[j].at[pl.ds(cut * height, height), :]
            target = out_ref.at[pl.ds(row + cut * height, height), pl.ds(column, WIDTH)]
            copies.append(pltpu.make_async_copy(source, target, sems.at[len(copies)]))
    for copy in copies:
        copy.start()
    for copy in copies:
        copy.wait()


def fill(places, blocks, weights=None, tile=False):
    anywhere = pl.BlockSpec(memory_space=pl.ANY)
    given = [] if weights is None else [weights]
    return pl.pallas_call(
        functools.partial(fill_kernel, places, len(blocks) + len(given)),
        out_shape=[pltpu.HBM((BLOCK, D), jnp.bfloat16)] + [jax.ShapeDtypeStruct((8, 128), jnp.float32)] * tile,
        in_specs=[anywhere] * len(blocks) + [anywhere] * len(given),
        out_specs=[anywhere] + [pl.BlockSpec((8, 128), lambda: (0, 0))] * tile,
        scratch_shapes=[pltpu.SemaphoreType.DMA((CUTS * len(blocks),))],
        input_output_aliases={len(blocks): 0} if given else {},
        compiler_params=pltpu.CompilerParams(vmem_limit_bytes=VMEM_BYTES),
        cost_estimate=pl.CostEstimate(flops=0, bytes_accessed=0, transcendentals=0),
    )(*map(in_vmem, blocks), *given)


def along_y(value):
    pairs = [(y * 2 + core, (y + 1 - 2 * core) % SIDE * 2 + core) for y in range(SIDE) for core in range(2)]
    return lax.ppermute(value, "fsdp", pairs)


def to_other_core(value):
    return lax.ppermute(value, "fsdp", [(i, i ^ 1) for i in range(8)])


def gather(low, state):
    one = along_y(low)
    other = to_other_core(low)
    one_other = along_y(other)
    one = after(one, state)
    two = along_y(one)
    one_swapped = to_other_core(one)
    halves = [to_other_core(one_other[row : row + PART]) for row in (0, PART)]
    near = ((0, False, 0), (0, True, 0), (1, False, 0), (1, True, 0), (-1, True, 0), (-1, False, 0), (-1, False, PART))
    weights, filled = fill(near, (low, other, one, one_other, one_swapped, *halves), tile=True)
    two = after(two, filled)
    two_swapped = to_other_core(two)
    weights = fill(((2, False, 0),), (two,), weights)[0]
    return fill(((2, True, 0),), (two_swapped,), weights)[0]


def on_device(grad_shards, hadamard_signs, scale_index, scale_table, master, mean_moment, var_moment):
    grad, scale_index, master, mean_moment, var_moment = map(in_hbm, (grad_shards[0], scale_index, master, mean_moment, var_moment))
    scale_table = in_hbm(scale_table)
    place = (lax.axis_index("dp") * 2 + (lax.axis_index("fsdp") & 1)).reshape(1)
    sign = in_hbm(hadamard_signs)
    hmat = in_hbm(jnp.asarray(hadamard(TILE)))
    *state, staged = stage(master, mean_moment, var_moment)
    terms = reduce_scatter(place, scale_table, sign, grad, scale_index, hmat, staged)
    plain, square = decode(place, scale_table, sign, terms, scale_index, hmat, lax.axis_size(("dp", "fsdp")))
    square = lax.all_to_all(square, ("dp", "fsdp"), 0, 0, tiled=True)
    state = [in_vmem(v) for v in (plain, *state)]
    low = adamw(weights_kernel, jax.ShapeDtypeStruct((BLOCK, WIDTH), jnp.bfloat16), square, *state)
    new_state = adamw(state_kernel, (jax.ShapeDtypeStruct(master.shape, jnp.float32),) * 3, square, *state)
    return *new_state, gather(low, in_hbm(new_state[0]))


def solution(mesh):
    return jax.shard_map(
        on_device,
        mesh=mesh,
        in_specs=(
            P("dp", None, "fsdp"),
            P("fsdp"),
            P("fsdp", None),
            P(),
            P("dp", "fsdp"),
            P("dp", "fsdp"),
            P("dp", "fsdp"),
        ),
        out_specs=(P("dp", "fsdp"), P("dp", "fsdp"), P("dp", "fsdp"), P("dp", None)),
        check_vma=False,
    )
```

```python
import functools
import math

import jax
import jax.numpy as jnp
import ml_dtypes
import numpy as np
from jax import lax
from jax.experimental import pallas as pl
from jax.experimental.pallas import tpu as pltpu
from jax.sharding import PartitionSpec as P

D = 6144
ROWS = 8192
TILE = 256
WIDTH = 768
TILES = WIDTH // TILE
SIDE = 4
BLOCK = 512
PART = 256
STEP = 128
ROOT_STEPS = 1450.0
CUTS = 4
RING0, RING1 = (2, 1), (3, 0)
LIMIT = 4.0 * math.sqrt(ROWS * D)
VMEM_BYTES = 14 * 1024 * 1024


def hadamard(length):
    index = np.arange(length)
    common_bits = index[:, None] & index[None, :]
    parity = np.zeros((length, length), np.int32)
    for bit_pos in range(length.bit_length() - 1):
        parity = parity ^ common_bits >> bit_pos & 1
    return (1 - 2 * parity).astype(ml_dtypes.bfloat16)


def hop(value, axis, step):
    pairs = []
    for device in range(128):
        x, z, core = device // 32, device // 8 % SIDE, device % 2
        if (axis == "first") == (core == 0):
            x = (x + step) % SIDE
        else:
            z = (z + step) % SIDE
        pairs.append((device, (x * SIDE + z) * 8 + device % 8))
    return lax.ppermute(value, ("dp", "fsdp"), pairs)


def in_hbm(value):
    return pltpu.with_memory_space_constraint(value, pltpu.HBM)


def in_vmem(value):
    return pltpu.with_memory_space_constraint(value, pltpu.VMEM)


def row_scales(index_refs, table_ref, inverse):
    index = jnp.concatenate([ref[...] for ref in index_refs], axis=1)
    scale = jnp.zeros(index.shape, jnp.float32)
    for level in range(table_ref.shape[0]):
        scale = jnp.where(index == level, table_ref[level], scale)
    if inverse:
        scale = 1.0 / (math.sqrt(TILE) * scale)
    ones = jnp.ones((8 - index.shape[0], index.shape[1]), jnp.float32)
    return jnp.concatenate([scale, ones], axis=0).T


def to_root(value):
    root = value * lax.rsqrt(jnp.maximum(jnp.abs(value), 1e-30)) * ROOT_STEPS
    return (root + jnp.where(root < 0, -0.5, 0.5)).astype(jnp.int32).astype(jnp.int16)


def from_root(root):
    root = root.astype(jnp.int32).astype(jnp.float32)
    return root * jnp.abs(root) * (1.0 / ROOT_STEPS**2)


def encode_kernel(counts, targets, ordered, place_ref, table_ref, sign_ref, hmat_ref, *refs):
    jobs = len(counts)
    outs = max(out for out, _ in targets) + 1
    inputs, outs = iter(refs[int(ordered) : -outs]), refs[-outs:]
    out_refs = [outs[out] if slot is None else outs[out].at[slot] for out, slot in targets]
    grad_refs, index_refs, arrived_refs = [], [], []
    for count in counts:
        grad_refs.append(next(inputs))
        index_refs.append(next(inputs))
        arrived_refs.append([next(inputs) for _ in range(count)])
    steps = row_scales(index_refs, table_ref, True)
    sign = (2 * sign_ref[...] - 1).reshape(1, WIDTH).astype(jnp.bfloat16)
    for tile in range(TILES):
        cols = slice(tile * TILE, (tile + 1) * TILE)
        signed = jnp.concatenate([ref[:, cols] for ref in grad_refs], axis=0) * sign[:, cols]
        rotated = jnp.dot(signed, hmat_ref[...], preferred_element_type=jnp.float32)
        codes = jnp.clip(rotated * steps[:, tile : tile + 1], -127.0, 127.0).astype(jnp.bfloat16)
        for job in range(jobs):
            code = codes[job * PART : (job + 1) * PART]
            if arrived_refs[job]:
                total = code.astype(jnp.float32)
                for ref in arrived_refs[job]:
                    total = total + ref[:, cols].astype(jnp.float32)
                code = to_root(total) if out_refs[job].dtype == jnp.int16 else total.astype(out_refs[job].dtype)
            out_refs[job][:, cols] = code


def block_at(place_ref, near, far):
    place = place_ref[0]
    x, z, core = place // (2 * SIDE), place // 2 % SIDE, place % 2
    x, z = x + jnp.where(core == 0, near, far), z + jnp.where(core == 0, far, near)
    return lax.rem(x, SIDE) * SIDE + lax.rem(z, SIDE)


def encode(place, table, sign, grad, index, hmat, grid, jobs, after=None):
    in_specs = [
        pl.BlockSpec(memory_space=pltpu.SMEM),
        pl.BlockSpec((WIDTH,), lambda *_: (0,)),
        pl.BlockSpec((TILE, TILE), lambda *_: (0, 0)),
    ]
    operands, out_specs, out_shape = [table, sign, hmat], [], []
    if after is not None:
        in_specs.append(pl.BlockSpec((8, 128), lambda *_: (0, 0)))
        operands.append(after)
    parts, targets = BLOCK // PART, []
    for near, far, arrived, spec, shape, dtype in jobs:
        rows = functools.partial(lambda near, far, i, j, place_ref: block_at(place_ref, near, far(i)) * parts + j, near, far)
        in_specs.append(pl.BlockSpec((PART, WIDTH), functools.partial(lambda rows, *at: (rows(*at), 0), rows)))
        in_specs.append(pl.BlockSpec((TILES, PART), functools.partial(lambda rows, *at: (0, rows(*at)), rows)))
        operands += [grad, index]
        for value, its_spec in arrived:
            in_specs.append(its_spec)
            operands.append(value)
        if spec is not None:
            out_specs.append(spec)
            out_shape.append(jax.ShapeDtypeStruct(shape, dtype))
        targets.append((len(out_specs) - 1, None if len(shape) == 2 else int(spec is None)))
    blocks = len(jobs) * grid[0] * parts
    return pl.pallas_call(
        functools.partial(encode_kernel, [len(job[2]) for job in jobs], targets, after is not None),
        out_shape=out_shape,
        grid_spec=pltpu.PrefetchScalarGridSpec(num_scalar_prefetch=1, grid=grid, in_specs=in_specs, out_specs=out_specs),
        compiler_params=pltpu.CompilerParams(vmem_limit_bytes=VMEM_BYTES),
        cost_estimate=pl.CostEstimate(flops=0, bytes_accessed=0, transcendentals=0),
    )(place, *operands)


def reduce_scatter(place, table, sign, grad, index, hmat, staged):
    code = functools.partial(encode, place, table, sign, grad, index, hmat)
    pair = ((2, BLOCK, WIDTH), jnp.bfloat16)
    both = pl.BlockSpec((2, PART, WIDTH), lambda i, j, place_ref: (0, j, 0))

    def round_of(*plan):
        jobs = []
        for _, near, ring in plan:
            jobs += [(near, lambda i, far=far: far, (), spec, *pair) for far, spec in zip(ring, (both, None), strict=True)]
        return [hop(v, "first", step) for v, (step, *_) in zip(code((1, BLOCK // PART), jobs), plan, strict=True)]

    up_far, down_far = round_of((1, 2, RING0), (-1, 2, RING1))
    up_own, down_own = round_of((1, 1, RING1), (-1, 3, RING0))
    single = pl.BlockSpec((PART, WIDTH), lambda i, j, place_ref: (j, 0))
    low = ((BLOCK, WIDTH), jnp.bfloat16)

    def of_slot(slot):
        return pl.BlockSpec((None, PART, WIDTH), lambda i, j, place_ref: (slot, j, 0))

    def sums_of(slot):
        plan = ((1, 1, RING0[slot], up_far), (-1, 3, RING1[slot], down_far))
        jobs = [(near, lambda i, far=far: far, [(v, of_slot(slot))], single, *low) for _, near, far, v in plan]
        return [hop(v, "first", step) for v, (step, *_) in zip(code((1, BLOCK // PART), jobs, staged), plan, strict=True)]

    def own_of(slot, *rings):
        plan, jobs = [], []
        for ring, whole in rings:
            far, part = (RING0[slot], down_own) if ring == 0 else (RING1[slot], up_own)
            shape = ((BLOCK, WIDTH), jnp.int16 if far else jnp.float32)
            jobs.append((0, lambda i, far=far: far, [(whole, single), (part, of_slot(slot))], single, *shape))
            plan.append(far)
        values = code((1, BLOCK // PART), jobs)
        return [in_vmem(hop(v, "second", far)) if far else v for v, far in zip(values, plan, strict=True)]

    early_up, early_down = sums_of(0)
    late_up, late_down = sums_of(1)
    two, three = own_of(0, (0, early_up), (1, early_down))
    (one,) = own_of(1, (0, late_up))
    (own,) = own_of(1, (1, late_down))
    return [own, two, one, three]


def decode_kernel(place_ref, table_ref, sign_ref, hmat_ref, own_ref, two_ref, one_ref, three_ref, index_ref, plain_ref, square_ref, sum_ref):
    f32 = jnp.float32

    @pl.when(pl.program_id(0) == 0)
    def _():
        sum_ref[...] = jnp.zeros_like(sum_ref)

    scales = row_scales([index_ref], table_ref, False) * (1.0 / math.sqrt(TILE))
    sign = (2 * sign_ref[...] - 1).reshape(1, WIDTH).astype(f32)
    square = sum_ref[...]
    for tile in range(TILES):
        cols = slice(tile * TILE, (tile + 1) * TILE)
        value = own_ref[:, cols] + from_root(two_ref[:, cols]) + from_root(one_ref[:, cols]) + from_root(three_ref[:, cols])
        plain = jnp.zeros(value.shape, f32)
        for _ in range(3):
            piece = value.astype(jnp.bfloat16)
            plain = plain + jnp.dot(piece, hmat_ref[...], preferred_element_type=f32)
            value = value - piece.astype(f32)
        plain = plain * scales[:, tile : tile + 1] * sign[:, cols]
        plain_ref[:, cols] = plain
        parts = jnp.sum((plain * plain).reshape(-1, 8, TILE), axis=0)
        square = square + parts[:, :128] + parts[:, 128:]
    sum_ref[...] = square
    square_ref[...] = jnp.broadcast_to(jnp.sum(square, axis=0, keepdims=True), square_ref.shape)


def decode(place, table, sign, terms, index, hmat, copies):
    parts = BLOCK // BLOCK
    single = pl.BlockSpec((BLOCK, WIDTH), lambda j, place_ref: (j, 0))
    return pl.pallas_call(
        decode_kernel,
        out_shape=(
            pltpu.VMEM((BLOCK, WIDTH), jnp.float32),
            pltpu.HBM((copies, 128), jnp.float32),
        ),
        grid_spec=pltpu.PrefetchScalarGridSpec(
            num_scalar_prefetch=1,
            grid=(parts,),
            in_specs=[
                pl.BlockSpec(memory_space=pltpu.SMEM),
                pl.BlockSpec((WIDTH,), lambda j, place_ref: (0,)),
                pl.BlockSpec((TILE, TILE), lambda j, place_ref: (0, 0)),
                *[single] * 4,
                pl.BlockSpec((TILES, BLOCK), lambda j, place_ref: (0, block_at(place_ref, 0, 0) * parts + j)),
            ],
            out_specs=(
                single,
                pl.BlockSpec((copies, 128), lambda j, place_ref: (0, 0)),
            ),
            scratch_shapes=[pltpu.VMEM((8, 128), jnp.float32)],
        ),
        compiler_params=pltpu.CompilerParams(vmem_limit_bytes=VMEM_BYTES),
        cost_estimate=pl.CostEstimate(flops=0, bytes_accessed=0, transcendentals=0),
    )(place, table, sign, hmat, *terms, index)


MEAN_SCALE = 0.02 / (1.0 - 0.9**10)
VAR_SCALE = 1.0 / (1.0 - 0.95**10)


def clip_factor(square_ref):
    square = jnp.sum(jnp.sum(square_ref[...], axis=0, keepdims=True), axis=1, keepdims=True)
    return LIMIT / jnp.maximum(jnp.sqrt(square), LIMIT)


def stepped(master, new_mean, new_var):
    spread = new_var * VAR_SCALE
    spread = spread * lax.rsqrt(spread)
    return 0.998 * master - new_mean * MEAN_SCALE / (spread + 1e-08)


def weights_kernel(square_ref, plain_ref, master_ref, mean_ref, var_ref, out_ref):
    grad = plain_ref[...] * clip_factor(square_ref)
    new_mean = 0.9 * mean_ref[...] + 0.1 * grad
    new_var = 0.95 * var_ref[...] + 0.05 * grad * grad
    out_ref[...] = stepped(master_ref[...], new_mean, new_var).astype(jnp.bfloat16)


def state_kernel(square_ref, plain_ref, master_ref, mean_ref, var_ref, new_master_ref, new_mean_ref, new_var_ref):
    grad = plain_ref[...] * clip_factor(square_ref)
    new_mean = 0.9 * mean_ref[...] + 0.1 * grad
    new_var = 0.95 * var_ref[...] + 0.05 * grad * grad
    new_mean_ref[...] = new_mean
    new_var_ref[...] = new_var
    new_master_ref[...] = stepped(master_ref[...], new_mean, new_var)


def adamw(kernel, out_shape, square, plain, master, mean, var):
    rows = pl.BlockSpec((STEP, WIDTH), lambda j: (j, 0))
    return pl.pallas_call(
        kernel,
        out_shape=out_shape,
        grid=(BLOCK // STEP,),
        in_specs=[pl.BlockSpec(square.shape, lambda j: (0, 0))] + [rows] * 4,
        out_specs=jax.tree.map(lambda _: rows, out_shape),
        compiler_params=pltpu.CompilerParams(vmem_limit_bytes=VMEM_BYTES),
        cost_estimate=pl.CostEstimate(flops=0, bytes_accessed=0, transcendentals=0),
    )(square, plain, master, mean, var)


def stage_kernel(*refs):
    for source, target in zip(refs[:3], refs[3:6], strict=True):
        target[...] = source[...]
    refs[6][...] = jnp.zeros_like(refs[6])


def stage(*state):
    rows = pl.BlockSpec((STEP, WIDTH), lambda j: (j, 0))
    return pl.pallas_call(
        stage_kernel,
        out_shape=[pltpu.VMEM(v.shape, v.dtype) for v in state] + [jax.ShapeDtypeStruct((8, 128), jnp.float32)],
        grid=(BLOCK // STEP,),
        in_specs=[rows] * 3,
        out_specs=[rows] * 3 + [pl.BlockSpec((8, 128), lambda j: (0, 0))],
        compiler_params=pltpu.CompilerParams(vmem_limit_bytes=VMEM_BYTES),
        cost_estimate=pl.CostEstimate(flops=0, bytes_accessed=0, transcendentals=0),
    )(*state)


def after(value, first):
    anywhere = pl.BlockSpec(memory_space=pl.ANY)
    return pl.pallas_call(
        lambda *_: None,
        out_shape=jax.ShapeDtypeStruct(value.shape, value.dtype),
        in_specs=[anywhere, anywhere],
        out_specs=anywhere,
        input_output_aliases={0: 0},
        compiler_params=pltpu.CompilerParams(vmem_limit_bytes=VMEM_BYTES),
    )(value, first)


def fill_kernel(places, out_at, *refs):
    out_ref, sems = refs[out_at], refs[-1]
    for tile_ref in refs[out_at + 1 : -1]:
        tile_ref[...] = jnp.zeros_like(tile_ref)
    at = lax.axis_index("fsdp")
    chip, core = at // 2, at % 2
    copies = []
    for j, (step, swapped, row) in enumerate(places):
        sender = (chip + SIDE - step + 2 * step * core) % SIDE
        column = pl.multiple_of((sender * 2 + (1 - core if swapped else core)) * WIDTH, WIDTH)
        height = refs[j].shape[0] // CUTS
        for cut in range(CUTS):
            source = refs[j].at[pl.ds(cut * height, height), :]
            target = out_ref.at[pl.ds(row + cut * height, height), pl.ds(column, WIDTH)]
            copies.append(pltpu.make_async_copy(source, target, sems.at[len(copies)]))
    for copy in copies:
        copy.start()
    for copy in copies:
        copy.wait()


def fill(places, blocks, weights=None, tile=False):
    anywhere = pl.BlockSpec(memory_space=pl.ANY)
    given = [] if weights is None else [weights]
    return pl.pallas_call(
        functools.partial(fill_kernel, places, len(blocks) + len(given)),
        out_shape=[pltpu.HBM((BLOCK, D), jnp.bfloat16)] + [jax.ShapeDtypeStruct((8, 128), jnp.float32)] * tile,
        in_specs=[anywhere] * len(blocks) + [anywhere] * len(given),
        out_specs=[anywhere] + [pl.BlockSpec((8, 128), lambda: (0, 0))] * tile,
        scratch_shapes=[pltpu.SemaphoreType.DMA((CUTS * len(blocks),))],
        input_output_aliases={len(blocks): 0} if given else {},
        compiler_params=pltpu.CompilerParams(vmem_limit_bytes=VMEM_BYTES),
        cost_estimate=pl.CostEstimate(flops=0, bytes_accessed=0, transcendentals=0),
    )(*map(in_vmem, blocks), *given)


def along_y(value):
    pairs = [(y * 2 + core, (y + 1 - 2 * core) % SIDE * 2 + core) for y in range(SIDE) for core in range(2)]
    return lax.ppermute(value, "fsdp", pairs)


def to_other_core(value):
    return lax.ppermute(value, "fsdp", [(i, i ^ 1) for i in range(8)])


def gather(low, state):
    one = along_y(low)
    other = to_other_core(low)
    one_other = along_y(other)
    one = after(one, state)
    two = along_y(one)
    one_swapped = to_other_core(one)
    halves = [to_other_core(one_other[row : row + PART]) for row in (0, PART)]
    near = ((0, False, 0), (0, True, 0), (1, False, 0), (1, True, 0), (-1, True, 0), (-1, False, 0), (-1, False, PART))
    weights, filled = fill(near, (low, other, one, one_other, one_swapped, *halves), tile=True)
    two = after(two, filled)
    two_swapped = to_other_core(two)
    weights = fill(((2, False, 0),), (two,), weights)[0]
    return fill(((2, True, 0),), (two_swapped,), weights)[0]


def on_device(grad_shards, hadamard_signs, scale_index, scale_table, master, mean_moment, var_moment):
    grad, scale_index, master, mean_moment, var_moment = map(in_hbm, (grad_shards[0], scale_index, master, mean_moment, var_moment))
    scale_table = in_hbm(scale_table)
    place = (lax.axis_index("dp") * 2 + (lax.axis_index("fsdp") & 1)).reshape(1)
    sign = in_hbm(hadamard_signs)
    hmat = in_hbm(jnp.asarray(hadamard(TILE)))
    *state, staged = stage(master, mean_moment, var_moment)
    terms = reduce_scatter(place, scale_table, sign, grad, scale_index, hmat, staged)
    plain, square = decode(place, scale_table, sign, terms, scale_index, hmat, lax.axis_size(("dp", "fsdp")))
    square = lax.all_to_all(square, ("dp", "fsdp"), 0, 0, tiled=True)
    state = [in_vmem(v) for v in (plain, *state)]
    low = adamw(weights_kernel, jax.ShapeDtypeStruct((BLOCK, WIDTH), jnp.bfloat16), square, *state)
    new_state = adamw(state_kernel, (jax.ShapeDtypeStruct(master.shape, jnp.float32),) * 3, square, *state)
    return *new_state, gather(low, in_hbm(new_state[0]))


def solution(mesh):
    return jax.shard_map(
        on_device,
        mesh=mesh,
        in_specs=(
            P("dp", None, "fsdp"),
            P("fsdp"),
            P("fsdp", None),
            P(),
            P("dp", "fsdp"),
            P("dp", "fsdp"),
            P("dp", "fsdp"),
        ),
        out_specs=(P("dp", "fsdp"), P("dp", "fsdp"), P("dp", "fsdp"), P("dp", None)),
        check_vma=False,
    )
```

```python
import functools
import math

import jax
import jax.numpy as jnp
import ml_dtypes
import numpy as np
from jax import lax
from jax.experimental import pallas as pl
from jax.experimental.pallas import tpu as pltpu
from jax.sharding import PartitionSpec as P

D = 6144
ROWS = 8192
TILE = 256
WIDTH = 768
TILES = WIDTH // TILE
SIDE = 4
BLOCK = 512
PART = 256
STEP = 128
ROOT_STEPS = 1450.0
CUTS = 4
RING0, RING1 = (2, 1), (3, 0)
LIMIT = 4.0 * math.sqrt(ROWS * D)
VMEM_BYTES = 14 * 1024 * 1024


def hadamard(length):
    index = np.arange(length)
    common_bits = index[:, None] & index[None, :]
    parity = np.zeros((length, length), np.int32)
    for bit_pos in range(length.bit_length() - 1):
        parity = parity ^ common_bits >> bit_pos & 1
    return (1 - 2 * parity).astype(ml_dtypes.bfloat16)


def hop(value, axis, step):
    pairs = []
    for device in range(128):
        x, z, core = device // 32, device // 8 % SIDE, device % 2
        if (axis == "first") == (core == 0):
            x = (x + step) % SIDE
        else:
            z = (z + step) % SIDE
        pairs.append((device, (x * SIDE + z) * 8 + device % 8))
    return lax.ppermute(value, ("dp", "fsdp"), pairs)


def in_hbm(value):
    return pltpu.with_memory_space_constraint(value, pltpu.HBM)


def in_vmem(value):
    return pltpu.with_memory_space_constraint(value, pltpu.VMEM)


def row_scales(index_refs, table_ref, inverse):
    index = jnp.concatenate([ref[...] for ref in index_refs], axis=1)
    scale = jnp.zeros(index.shape, jnp.float32)
    for level in range(table_ref.shape[0]):
        scale = jnp.where(index == level, table_ref[level], scale)
    if inverse:
        scale = 1.0 / (math.sqrt(TILE) * scale)
    ones = jnp.ones((8 - index.shape[0], index.shape[1]), jnp.float32)
    return jnp.concatenate([scale, ones], axis=0).T


def to_root(value):
    root = value * lax.rsqrt(jnp.maximum(jnp.abs(value), 1e-30)) * ROOT_STEPS
    return jnp.round(root).astype(jnp.int32).astype(jnp.int16)


def from_root(root):
    root = root.astype(jnp.int32).astype(jnp.float32)
    return root * jnp.abs(root) * (1.0 / ROOT_STEPS**2)


def encode_kernel(counts, targets, ordered, place_ref, table_ref, sign_ref, hmat_ref, *refs):
    jobs = len(counts)
    outs = max(out for out, _ in targets) + 1
    inputs, outs = iter(refs[int(ordered) : -outs]), refs[-outs:]
    out_refs = [outs[out] if slot is None else outs[out].at[slot] for out, slot in targets]
    grad_refs, index_refs, arrived_refs = [], [], []
    for count in counts:
        grad_refs.append(next(inputs))
        index_refs.append(next(inputs))
        arrived_refs.append([next(inputs) for _ in range(count)])
    steps = row_scales(index_refs, table_ref, True)
    sign = (2 * sign_ref[...] - 1).reshape(1, WIDTH).astype(jnp.bfloat16)
    for tile in range(TILES):
        cols = slice(tile * TILE, (tile + 1) * TILE)
        signed = jnp.concatenate([ref[:, cols] for ref in grad_refs], axis=0) * sign[:, cols]
        rotated = jnp.dot(signed, hmat_ref[...], preferred_element_type=jnp.float32)
        codes = jnp.clip(rotated * steps[:, tile : tile + 1], -127.0, 127.0).astype(jnp.bfloat16)
        for job in range(jobs):
            code = codes[job * PART : (job + 1) * PART]
            if arrived_refs[job]:
                total = code.astype(jnp.float32)
                for ref in arrived_refs[job]:
                    total = total + ref[:, cols].astype(jnp.float32)
                code = to_root(total) if out_refs[job].dtype == jnp.int16 else total.astype(out_refs[job].dtype)
            out_refs[job][:, cols] = code


def block_at(place_ref, near, far):
    place = place_ref[0]
    x, z, core = place // (2 * SIDE), place // 2 % SIDE, place % 2
    x, z = x + jnp.where(core == 0, near, far), z + jnp.where(core == 0, far, near)
    return lax.rem(x, SIDE) * SIDE + lax.rem(z, SIDE)


def encode(place, table, sign, grad, index, hmat, grid, jobs, after=None):
    in_specs = [
        pl.BlockSpec(memory_space=pltpu.SMEM),
        pl.BlockSpec((WIDTH,), lambda *_: (0,)),
        pl.BlockSpec((TILE, TILE), lambda *_: (0, 0)),
    ]
    operands, out_specs, out_shape = [table, sign, hmat], [], []
    if after is not None:
        in_specs.append(pl.BlockSpec((8, 128), lambda *_: (0, 0)))
        operands.append(after)
    parts, targets = BLOCK // PART, []
    for near, far, arrived, spec, shape, dtype in jobs:
        rows = functools.partial(lambda near, far, i, j, place_ref: block_at(place_ref, near, far(i)) * parts + j, near, far)
        in_specs.append(pl.BlockSpec((PART, WIDTH), functools.partial(lambda rows, *at: (rows(*at), 0), rows)))
        in_specs.append(pl.BlockSpec((TILES, PART), functools.partial(lambda rows, *at: (0, rows(*at)), rows)))
        operands += [grad, index]
        for value, its_spec in arrived:
            in_specs.append(its_spec)
            operands.append(value)
        if spec is not None:
            out_specs.append(spec)
            out_shape.append(jax.ShapeDtypeStruct(shape, dtype))
        targets.append((len(out_specs) - 1, None if len(shape) == 2 else int(spec is None)))
    blocks = len(jobs) * grid[0] * parts
    return pl.pallas_call(
        functools.partial(encode_kernel, [len(job[2]) for job in jobs], targets, after is not None),
        out_shape=out_shape,
        grid_spec=pltpu.PrefetchScalarGridSpec(num_scalar_prefetch=1, grid=grid, in_specs=in_specs, out_specs=out_specs),
        compiler_params=pltpu.CompilerParams(vmem_limit_bytes=VMEM_BYTES),
        cost_estimate=pl.CostEstimate(flops=0, bytes_accessed=0, transcendentals=0),
    )(place, *operands)


def reduce_scatter(place, table, sign, grad, index, hmat, staged):
    code = functools.partial(encode, place, table, sign, grad, index, hmat)
    pair = ((2, BLOCK, WIDTH), jnp.bfloat16)
    both = pl.BlockSpec((2, PART, WIDTH), lambda i, j, place_ref: (0, j, 0))

    def round_of(*plan):
        jobs = []
        for _, near, ring in plan:
            jobs += [(near, lambda i, far=far: far, (), spec, *pair) for far, spec in zip(ring, (both, None), strict=True)]
        return [hop(v, "first", step) for v, (step, *_) in zip(code((1, BLOCK // PART), jobs), plan, strict=True)]

    up_far, down_far = round_of((1, 2, RING0), (-1, 2, RING1))
    up_own, down_own = round_of((1, 1, RING1), (-1, 3, RING0))
    single = pl.BlockSpec((PART, WIDTH), lambda i, j, place_ref: (j, 0))
    low = ((BLOCK, WIDTH), jnp.bfloat16)

    def of_slot(slot):
        return pl.BlockSpec((None, PART, WIDTH), lambda i, j, place_ref: (slot, j, 0))

    def sums_of(slot):
        plan = ((1, 1, RING0[slot], up_far), (-1, 3, RING1[slot], down_far))
        jobs = [(near, lambda i, far=far: far, [(v, of_slot(slot))], single, *low) for _, near, far, v in plan]
        return [hop(v, "first", step) for v, (step, *_) in zip(code((1, BLOCK // PART), jobs, staged), plan, strict=True)]

    def own_of(slot, *rings):
        plan, jobs = [], []
        for ring, whole in rings:
            far, part = (RING0[slot], down_own) if ring == 0 else (RING1[slot], up_own)
            shape = ((BLOCK, WIDTH), jnp.int16 if far else jnp.float32)
            jobs.append((0, lambda i, far=far: far, [(whole, single), (part, of_slot(slot))], single, *shape))
            plan.append(far)
        values = code((1, BLOCK // PART), jobs)
        return [in_vmem(hop(v, "second", far)) if far else v for v, far in zip(values, plan, strict=True)]

    early_up, early_down = sums_of(0)
    late_up, late_down = sums_of(1)
    two, three = own_of(0, (0, early_up), (1, early_down))
    (one,) = own_of(1, (0, late_up))
    (own,) = own_of(1, (1, late_down))
    return [own, two, one, three]


def decode_kernel(place_ref, table_ref, sign_ref, hmat_ref, own_ref, two_ref, one_ref, three_ref, index_ref, plain_ref, square_ref, sum_ref):
    f32 = jnp.float32

    @pl.when(pl.program_id(0) == 0)
    def _():
        sum_ref[...] = jnp.zeros_like(sum_ref)

    scales = row_scales([index_ref], table_ref, False) * (1.0 / math.sqrt(TILE))
    sign = (2 * sign_ref[...] - 1).reshape(1, WIDTH).astype(f32)
    square = sum_ref[...]
    for tile in range(TILES):
        cols = slice(tile * TILE, (tile + 1) * TILE)
        value = own_ref[:, cols] + from_root(two_ref[:, cols]) + from_root(one_ref[:, cols]) + from_root(three_ref[:, cols])
        plain = jnp.zeros(value.shape, f32)
        for _ in range(3):
            piece = value.astype(jnp.bfloat16)
            plain = plain + jnp.dot(piece, hmat_ref[...], preferred_element_type=f32)
            value = value - piece.astype(f32)
        plain = plain * scales[:, tile : tile + 1] * sign[:, cols]
        plain_ref[:, cols] = plain
        parts = jnp.sum((plain * plain).reshape(-1, 8, TILE), axis=0)
        square = square + parts[:, :128] + parts[:, 128:]
    sum_ref[...] = square
    square_ref[...] = jnp.broadcast_to(jnp.sum(square, axis=0, keepdims=True), square_ref.shape)


def decode(place, table, sign, terms, index, hmat, copies):
    parts = BLOCK // BLOCK
    single = pl.BlockSpec((BLOCK, WIDTH), lambda j, place_ref: (j, 0))
    return pl.pallas_call(
        decode_kernel,
        out_shape=(
            pltpu.VMEM((BLOCK, WIDTH), jnp.float32),
            pltpu.HBM((copies, 128), jnp.float32),
        ),
        grid_spec=pltpu.PrefetchScalarGridSpec(
            num_scalar_prefetch=1,
            grid=(parts,),
            in_specs=[
                pl.BlockSpec(memory_space=pltpu.SMEM),
                pl.BlockSpec((WIDTH,), lambda j, place_ref: (0,)),
                pl.BlockSpec((TILE, TILE), lambda j, place_ref: (0, 0)),
                *[single] * 4,
                pl.BlockSpec((TILES, BLOCK), lambda j, place_ref: (0, block_at(place_ref, 0, 0) * parts + j)),
            ],
            out_specs=(
                single,
                pl.BlockSpec((copies, 128), lambda j, place_ref: (0, 0)),
            ),
            scratch_shapes=[pltpu.VMEM((8, 128), jnp.float32)],
        ),
        compiler_params=pltpu.CompilerParams(vmem_limit_bytes=VMEM_BYTES),
        cost_estimate=pl.CostEstimate(flops=0, bytes_accessed=0, transcendentals=0),
    )(place, table, sign, hmat, *terms, index)


MEAN_SCALE = 0.02 / (1.0 - 0.9**10)
VAR_SCALE = 1.0 / (1.0 - 0.95**10)


def clip_factor(square_ref):
    square = jnp.sum(jnp.sum(square_ref[...], axis=0, keepdims=True), axis=1, keepdims=True)
    return LIMIT / jnp.maximum(jnp.sqrt(square), LIMIT)


def stepped(master, new_mean, new_var):
    spread = new_var * VAR_SCALE
    spread = spread * lax.rsqrt(spread)
    return 0.998 * master - new_mean * MEAN_SCALE / (spread + 1e-08)


def weights_kernel(square_ref, plain_ref, master_ref, mean_ref, var_ref, out_ref):
    grad = plain_ref[...] * clip_factor(square_ref)
    new_mean = 0.9 * mean_ref[...] + 0.1 * grad
    new_var = 0.95 * var_ref[...] + 0.05 * grad * grad
    out_ref[...] = stepped(master_ref[...], new_mean, new_var).astype(jnp.bfloat16)


def state_kernel(square_ref, plain_ref, master_ref, mean_ref, var_ref, new_master_ref, new_mean_ref, new_var_ref):
    grad = plain_ref[...] * clip_factor(square_ref)
    new_mean = 0.9 * mean_ref[...] + 0.1 * grad
    new_var = 0.95 * var_ref[...] + 0.05 * grad * grad
    new_mean_ref[...] = new_mean
    new_var_ref[...] = new_var
    new_master_ref[...] = stepped(master_ref[...], new_mean, new_var)


def adamw(kernel, out_shape, square, plain, master, mean, var):
    rows = pl.BlockSpec((STEP, WIDTH), lambda j: (j, 0))
    return pl.pallas_call(
        kernel,
        out_shape=out_shape,
        grid=(BLOCK // STEP,),
        in_specs=[pl.BlockSpec(square.shape, lambda j: (0, 0))] + [rows] * 4,
        out_specs=jax.tree.map(lambda _: rows, out_shape),
        compiler_params=pltpu.CompilerParams(vmem_limit_bytes=VMEM_BYTES),
        cost_estimate=pl.CostEstimate(flops=0, bytes_accessed=0, transcendentals=0),
    )(square, plain, master, mean, var)


def stage_kernel(*refs):
    for source, target in zip(refs[:3], refs[3:6], strict=True):
        target[...] = source[...]
    refs[6][...] = jnp.zeros_like(refs[6])


def stage(*state):
    rows = pl.BlockSpec((STEP, WIDTH), lambda j: (j, 0))
    return pl.pallas_call(
        stage_kernel,
        out_shape=[pltpu.VMEM(v.shape, v.dtype) for v in state] + [jax.ShapeDtypeStruct((8, 128), jnp.float32)],
        grid=(BLOCK // STEP,),
        in_specs=[rows] * 3,
        out_specs=[rows] * 3 + [pl.BlockSpec((8, 128), lambda j: (0, 0))],
        compiler_params=pltpu.CompilerParams(vmem_limit_bytes=VMEM_BYTES),
        cost_estimate=pl.CostEstimate(flops=0, bytes_accessed=0, transcendentals=0),
    )(*state)


def after(value, first):
    anywhere = pl.BlockSpec(memory_space=pl.ANY)
    return pl.pallas_call(
        lambda *_: None,
        out_shape=jax.ShapeDtypeStruct(value.shape, value.dtype),
        in_specs=[anywhere, anywhere],
        out_specs=anywhere,
        input_output_aliases={0: 0},
        compiler_params=pltpu.CompilerParams(vmem_limit_bytes=VMEM_BYTES),
    )(value, first)


def fill_kernel(places, out_at, *refs):
    out_ref, sems = refs[out_at], refs[-1]
    for tile_ref in refs[out_at + 1 : -1]:
        tile_ref[...] = jnp.zeros_like(tile_ref)
    at = lax.axis_index("fsdp")
    chip, core = at // 2, at % 2
    copies = []
    for j, (step, swapped, row) in enumerate(places):
        sender = (chip + SIDE - step + 2 * step * core) % SIDE
        column = pl.multiple_of((sender * 2 + (1 - core if swapped else core)) * WIDTH, WIDTH)
        height = refs[j].shape[0] // CUTS
        for cut in range(CUTS):
            source = refs[j].at[pl.ds(cut * height, height), :]
            target = out_ref.at[pl.ds(row + cut * height, height), pl.ds(column, WIDTH)]
            copies.append(pltpu.make_async_copy(source, target, sems.at[len(copies)]))
    for copy in copies:
        copy.start()
    for copy in copies:
        copy.wait()


def fill(places, blocks, weights=None, tile=False):
    anywhere = pl.BlockSpec(memory_space=pl.ANY)
    given = [] if weights is None else [weights]
    return pl.pallas_call(
        functools.partial(fill_kernel, places, len(blocks) + len(given)),
        out_shape=[pltpu.HBM((BLOCK, D), jnp.bfloat16)] + [jax.ShapeDtypeStruct((8, 128), jnp.float32)] * tile,
        in_specs=[anywhere] * len(blocks) + [anywhere] * len(given),
        out_specs=[anywhere] + [pl.BlockSpec((8, 128), lambda: (0, 0))] * tile,
        scratch_shapes=[pltpu.SemaphoreType.DMA((CUTS * len(blocks),))],
        input_output_aliases={len(blocks): 0} if given else {},
        compiler_params=pltpu.CompilerParams(vmem_limit_bytes=VMEM_BYTES),
        cost_estimate=pl.CostEstimate(flops=0, bytes_accessed=0, transcendentals=0),
    )(*map(in_vmem, blocks), *given)


def along_y(value):
    pairs = [(y * 2 + core, (y + 1 - 2 * core) % SIDE * 2 + core) for y in range(SIDE) for core in range(2)]
    return lax.ppermute(value, "fsdp", pairs)


def to_other_core(value):
    return lax.ppermute(value, "fsdp", [(i, i ^ 1) for i in range(8)])


def gather(low, state):
    one = along_y(low)
    other = to_other_core(low)
    one_other = along_y(other)
    one = after(one, state)
    two = along_y(one)
    one_swapped = to_other_core(one)
    halves = [to_other_core(one_other[row : row + PART]) for row in (0, PART)]
    near = ((0, False, 0), (0, True, 0), (1, False, 0), (1, True, 0), (-1, True, 0), (-1, False, 0), (-1, False, PART))
    weights, filled = fill(near, (low, other, one, one_other, one_swapped, *halves), tile=True)
    two = after(two, filled)
    two_swapped = to_other_core(two)
    weights = fill(((2, False, 0),), (two,), weights)[0]
    return fill(((2, True, 0),), (two_swapped,), weights)[0]


def on_device(grad_shards, hadamard_signs, scale_index, scale_table, master, mean_moment, var_moment):
    grad, scale_index, master, mean_moment, var_moment = map(in_hbm, (grad_shards[0], scale_index, master, mean_moment, var_moment))
    scale_table = in_hbm(scale_table)
    place = (lax.axis_index("dp") * 2 + (lax.axis_index("fsdp") & 1)).reshape(1)
    sign = in_hbm(hadamard_signs)
    hmat = in_hbm(jnp.asarray(hadamard(TILE)))
    *state, staged = stage(master, mean_moment, var_moment)
    terms = reduce_scatter(place, scale_table, sign, grad, scale_index, hmat, staged)
    plain, square = decode(place, scale_table, sign, terms, scale_index, hmat, lax.axis_size(("dp", "fsdp")))
    square = lax.all_to_all(square, ("dp", "fsdp"), 0, 0, tiled=True)
    state = [in_vmem(v) for v in (plain, *state)]
    low = adamw(weights_kernel, jax.ShapeDtypeStruct((BLOCK, WIDTH), jnp.bfloat16), square, *state)
    new_state = adamw(state_kernel, (jax.ShapeDtypeStruct(master.shape, jnp.float32),) * 3, square, *state)
    return *new_state, gather(low, in_hbm(new_state[0]))


def solution(mesh):
    return jax.shard_map(
        on_device,
        mesh=mesh,
        in_specs=(
            P("dp", None, "fsdp"),
            P("fsdp"),
            P("fsdp", None),
            P(),
            P("dp", "fsdp"),
            P("dp", "fsdp"),
            P("dp", "fsdp"),
        ),
        out_specs=(P("dp", "fsdp"), P("dp", "fsdp"), P("dp", "fsdp"), P("dp", None)),
        check_vma=False,
    )
```

```python
import functools
import math

import jax
import jax.numpy as jnp
import ml_dtypes
import numpy as np
from jax import lax
from jax.experimental import pallas as pl
from jax.experimental.pallas import tpu as pltpu
from jax.sharding import PartitionSpec as P

D = 6144
ROWS = 8192
TILE = 256
WIDTH = 768
TILES = WIDTH // TILE
SIDE = 4
BLOCK = 512
PART = 256
STEP = 128
ROOT_STEPS = 1450.0
CUTS = 4
RING0, RING1 = (2, 1), (3, 0)
LIMIT = 4.0 * math.sqrt(ROWS * D)
VMEM_BYTES = 14 * 1024 * 1024


def hadamard(length):
    index = np.arange(length)
    common_bits = index[:, None] & index[None, :]
    parity = np.zeros((length, length), np.int32)
    for bit_pos in range(length.bit_length() - 1):
        parity = parity ^ common_bits >> bit_pos & 1
    return (1 - 2 * parity).astype(ml_dtypes.bfloat16)


def hop(value, axis, step):
    pairs = []
    for device in range(128):
        x, z, core = device // 32, device // 8 % SIDE, device % 2
        if (axis == "first") == (core == 0):
            x = (x + step) % SIDE
        else:
            z = (z + step) % SIDE
        pairs.append((device, (x * SIDE + z) * 8 + device % 8))
    return lax.ppermute(value, ("dp", "fsdp"), pairs)


def in_hbm(value):
    return pltpu.with_memory_space_constraint(value, pltpu.HBM)


def in_vmem(value):
    return pltpu.with_memory_space_constraint(value, pltpu.VMEM)


def row_scales(index_refs, table_ref, inverse):
    index = jnp.concatenate([ref[...] for ref in index_refs], axis=1)
    scale = jnp.zeros(index.shape, jnp.float32)
    for level in range(table_ref.shape[0]):
        scale = jnp.where(index == level, table_ref[level], scale)
    if inverse:
        scale = 1.0 / (math.sqrt(TILE) * scale)
    ones = jnp.ones((8 - index.shape[0], index.shape[1]), jnp.float32)
    return jnp.concatenate([scale, ones], axis=0).T


def to_root(value):
    root = value * lax.rsqrt(jnp.maximum(jnp.abs(value), 1e-30)) * ROOT_STEPS
    return jnp.round(root).astype(jnp.int32).astype(jnp.int16)


def from_root(root):
    root = root.astype(jnp.int32).astype(jnp.float32)
    return root * jnp.abs(root) * (1.0 / ROOT_STEPS**2)


def encode_kernel(counts, targets, ordered, place_ref, table_ref, sign_ref, hmat_ref, *refs):
    jobs = len(counts)
    outs = max(out for out, _ in targets) + 1
    inputs, outs = iter(refs[int(ordered) : -outs]), refs[-outs:]
    out_refs = [outs[out] if slot is None else outs[out].at[slot] for out, slot in targets]
    grad_refs, index_refs, arrived_refs = [], [], []
    for count in counts:
        grad_refs.append(next(inputs))
        index_refs.append(next(inputs))
        arrived_refs.append([next(inputs) for _ in range(count)])
    steps = row_scales(index_refs, table_ref, True)
    sign = (2 * sign_ref[...] - 1).reshape(1, WIDTH).astype(jnp.bfloat16)
    for tile in range(TILES):
        cols = slice(tile * TILE, (tile + 1) * TILE)
        signed = jnp.concatenate([ref[:, cols] for ref in grad_refs], axis=0) * sign[:, cols]
        rotated = jnp.dot(signed, hmat_ref[...], preferred_element_type=jnp.float32)
        codes = jnp.clip(rotated * steps[:, tile : tile + 1], -127.0, 127.0).astype(jnp.bfloat16)
        for job in range(jobs):
            code = codes[job * PART : (job + 1) * PART]
            if arrived_refs[job]:
                total = code.astype(jnp.float32)
                for ref in arrived_refs[job]:
                    total = total + ref[:, cols].astype(jnp.float32)
                code = to_root(total) if out_refs[job].dtype == jnp.int16 else total.astype(out_refs[job].dtype)
            out_refs[job][:, cols] = code


def block_at(place_ref, near, far):
    place = place_ref[0]
    x, z, core = place // (2 * SIDE), place // 2 % SIDE, place % 2
    x, z = x + jnp.where(core == 0, near, far), z + jnp.where(core == 0, far, near)
    return lax.rem(x, SIDE) * SIDE + lax.rem(z, SIDE)


def encode(place, table, sign, grad, index, hmat, grid, jobs, after=None):
    in_specs = [
        pl.BlockSpec(memory_space=pltpu.SMEM),
        pl.BlockSpec((WIDTH,), lambda *_: (0,)),
        pl.BlockSpec((TILE, TILE), lambda *_: (0, 0)),
    ]
    operands, out_specs, out_shape = [table, sign, hmat], [], []
    if after is not None:
        in_specs.append(pl.BlockSpec((8, 128), lambda *_: (0, 0)))
        operands.append(after)
    parts, targets = BLOCK // PART, []
    for near, far, arrived, spec, shape, dtype in jobs:
        rows = functools.partial(lambda near, far, i, j, place_ref: block_at(place_ref, near, far(i)) * parts + j, near, far)
        in_specs.append(pl.BlockSpec((PART, WIDTH), functools.partial(lambda rows, *at: (rows(*at), 0), rows)))
        in_specs.append(pl.BlockSpec((TILES, PART), functools.partial(lambda rows, *at: (0, rows(*at)), rows)))
        operands += [grad, index]
        for value, its_spec in arrived:
            in_specs.append(its_spec)
            operands.append(value)
        if spec is not None:
            out_specs.append(spec)
            out_shape.append(jax.ShapeDtypeStruct(shape, dtype))
        targets.append((len(out_specs) - 1, None if len(shape) == 2 else int(spec is None)))
    blocks = len(jobs) * grid[0] * parts
    return pl.pallas_call(
        functools.partial(encode_kernel, [len(job[2]) for job in jobs], targets, after is not None),
        out_shape=out_shape,
        grid_spec=pltpu.PrefetchScalarGridSpec(num_scalar_prefetch=1, grid=grid, in_specs=in_specs, out_specs=out_specs),
        compiler_params=pltpu.CompilerParams(vmem_limit_bytes=VMEM_BYTES),
        cost_estimate=pl.CostEstimate(flops=0, bytes_accessed=0, transcendentals=0),
    )(place, *operands)


def reduce_scatter(place, table, sign, grad, index, hmat, staged):
    code = functools.partial(encode, place, table, sign, grad, index, hmat)
    pair = ((2, BLOCK, WIDTH), jnp.bfloat16)
    both = pl.BlockSpec((2, PART, WIDTH), lambda i, j, place_ref: (0, j, 0))

    def round_of(*plan):
        jobs = []
        for _, near, ring in plan:
            jobs += [(near, lambda i, far=far: far, (), spec, *pair) for far, spec in zip(ring, (both, None), strict=True)]
        return [hop(v, "first", step) for v, (step, *_) in zip(code((1, BLOCK // PART), jobs), plan, strict=True)]

    up_far, down_far = round_of((1, 2, RING0), (-1, 2, RING1))
    up_own, down_own = round_of((1, 1, RING1), (-1, 3, RING0))
    single = pl.BlockSpec((PART, WIDTH), lambda i, j, place_ref: (j, 0))
    low = ((BLOCK, WIDTH), jnp.bfloat16)

    def of_slot(slot):
        return pl.BlockSpec((None, PART, WIDTH), lambda i, j, place_ref: (slot, j, 0))

    def sums_of(slot):
        plan = ((1, 1, RING0[slot], up_far), (-1, 3, RING1[slot], down_far))
        jobs = [(near, lambda i, far=far: far, [(v, of_slot(slot))], single, *low) for _, near, far, v in plan]
        return [hop(v, "first", step) for v, (step, *_) in zip(code((1, BLOCK // PART), jobs, staged), plan, strict=True)]

    def own_of(slot, *rings):
        plan, jobs = [], []
        for ring, whole in rings:
            far, part = (RING0[slot], down_own) if ring == 0 else (RING1[slot], up_own)
            shape = ((BLOCK, WIDTH), jnp.int16 if far else jnp.float32)
            jobs.append((0, lambda i, far=far: far, [(whole, single), (part, of_slot(slot))], single, *shape))
            plan.append(far)
        values = code((1, BLOCK // PART), jobs)
        return [in_vmem(hop(v, "second", far)) if far else v for v, far in zip(values, plan, strict=True)]

    early_up, early_down = sums_of(0)
    late_up, late_down = sums_of(1)
    two, three = own_of(0, (0, early_up), (1, early_down))
    (one,) = own_of(1, (0, late_up))
    (own,) = own_of(1, (1, late_down))
    return [own, two, one, three]


def decode_kernel(place_ref, table_ref, sign_ref, hmat_ref, own_ref, two_ref, one_ref, three_ref, index_ref, plain_ref, square_ref, sum_ref):
    f32 = jnp.float32

    @pl.when(pl.program_id(0) == 0)
    def _():
        sum_ref[...] = jnp.zeros_like(sum_ref)

    scales = row_scales([index_ref], table_ref, False) * (1.0 / math.sqrt(TILE))
    sign = (2 * sign_ref[...] - 1).reshape(1, WIDTH).astype(f32)
    square = sum_ref[...]
    for tile in range(TILES):
        cols = slice(tile * TILE, (tile + 1) * TILE)
        value = own_ref[:, cols] + from_root(two_ref[:, cols]) + from_root(one_ref[:, cols]) + from_root(three_ref[:, cols])
        plain = jnp.zeros(value.shape, f32)
        for _ in range(3):
            piece = value.astype(jnp.bfloat16)
            plain = plain + jnp.dot(piece, hmat_ref[...], preferred_element_type=f32)
            value = value - piece.astype(f32)
        plain = plain * scales[:, tile : tile + 1] * sign[:, cols]
        plain_ref[:, cols] = plain
        parts = jnp.sum((plain * plain).reshape(-1, 8, TILE), axis=0)
        square = square + parts[:, :128] + parts[:, 128:]
    sum_ref[...] = square
    square_ref[...] = jnp.broadcast_to(jnp.sum(square, axis=0, keepdims=True), square_ref.shape)


def decode(place, table, sign, terms, index, hmat, copies):
    parts = BLOCK // BLOCK
    single = pl.BlockSpec((BLOCK, WIDTH), lambda j, place_ref: (j, 0))
    return pl.pallas_call(
        decode_kernel,
        out_shape=(
            pltpu.VMEM((BLOCK, WIDTH), jnp.float32),
            pltpu.HBM((copies, 128), jnp.float32),
        ),
        grid_spec=pltpu.PrefetchScalarGridSpec(
            num_scalar_prefetch=1,
            grid=(parts,),
            in_specs=[
                pl.BlockSpec(memory_space=pltpu.SMEM),
                pl.BlockSpec((WIDTH,), lambda j, place_ref: (0,)),
                pl.BlockSpec((TILE, TILE), lambda j, place_ref: (0, 0)),
                *[single] * 4,
                pl.BlockSpec((TILES, BLOCK), lambda j, place_ref: (0, block_at(place_ref, 0, 0) * parts + j)),
            ],
            out_specs=(
                single,
                pl.BlockSpec((copies, 128), lambda j, place_ref: (0, 0)),
            ),
            scratch_shapes=[pltpu.VMEM((8, 128), jnp.float32)],
        ),
        compiler_params=pltpu.CompilerParams(vmem_limit_bytes=VMEM_BYTES),
        cost_estimate=pl.CostEstimate(flops=0, bytes_accessed=0, transcendentals=0),
    )(place, table, sign, hmat, *terms, index)


MEAN_SCALE = 0.02 / (1.0 - 0.9**10)
VAR_SCALE = 1.0 / (1.0 - 0.95**10)


def clip_factor(square_ref, factor_ref):
    @pl.when(pl.program_id(0) == 0)
    def _():
        square = jnp.sum(jnp.sum(square_ref[...], axis=0, keepdims=True), axis=1, keepdims=True)
        factor_ref[...] = jnp.broadcast_to(LIMIT / jnp.maximum(jnp.sqrt(square), LIMIT), factor_ref.shape)

    return factor_ref[...]


def stepped(master, new_mean, new_var):
    spread = new_var * VAR_SCALE
    spread = spread * lax.rsqrt(spread)
    return 0.998 * master - new_mean * MEAN_SCALE / (spread + 1e-08)


def weights_kernel(square_ref, plain_ref, master_ref, mean_ref, var_ref, out_ref, factor_ref):
    grad = plain_ref[...] * clip_factor(square_ref, factor_ref)
    new_mean = 0.9 * mean_ref[...] + 0.1 * grad
    new_var = 0.95 * var_ref[...] + 0.05 * grad * grad
    out_ref[...] = stepped(master_ref[...], new_mean, new_var).astype(jnp.bfloat16)


def state_kernel(square_ref, plain_ref, master_ref, mean_ref, var_ref, new_master_ref, new_mean_ref, new_var_ref, factor_ref):
    grad = plain_ref[...] * clip_factor(square_ref, factor_ref)
    new_mean = 0.9 * mean_ref[...] + 0.1 * grad
    new_var = 0.95 * var_ref[...] + 0.05 * grad * grad
    new_mean_ref[...] = new_mean
    new_var_ref[...] = new_var
    new_master_ref[...] = stepped(master_ref[...], new_mean, new_var)


def adamw(kernel, out_shape, square, plain, master, mean, var):
    rows = pl.BlockSpec((STEP, WIDTH), lambda j: (j, 0))
    return pl.pallas_call(
        kernel,
        out_shape=out_shape,
        grid=(BLOCK // STEP,),
        in_specs=[pl.BlockSpec(square.shape, lambda j: (0, 0))] + [rows] * 4,
        out_specs=jax.tree.map(lambda _: rows, out_shape),
        scratch_shapes=[pltpu.VMEM((1, WIDTH), jnp.float32)],
        compiler_params=pltpu.CompilerParams(vmem_limit_bytes=VMEM_BYTES),
        cost_estimate=pl.CostEstimate(flops=0, bytes_accessed=0, transcendentals=0),
    )(square, plain, master, mean, var)


def stage_kernel(*refs):
    for source, target in zip(refs[:3], refs[3:6], strict=True):
        target[...] = source[...]
    refs[6][...] = jnp.zeros_like(refs[6])


def stage(*state):
    rows = pl.BlockSpec((STEP, WIDTH), lambda j: (j, 0))
    return pl.pallas_call(
        stage_kernel,
        out_shape=[pltpu.VMEM(v.shape, v.dtype) for v in state] + [jax.ShapeDtypeStruct((8, 128), jnp.float32)],
        grid=(BLOCK // STEP,),
        in_specs=[rows] * 3,
        out_specs=[rows] * 3 + [pl.BlockSpec((8, 128), lambda j: (0, 0))],
        compiler_params=pltpu.CompilerParams(vmem_limit_bytes=VMEM_BYTES),
        cost_estimate=pl.CostEstimate(flops=0, bytes_accessed=0, transcendentals=0),
    )(*state)


def after(value, first):
    anywhere = pl.BlockSpec(memory_space=pl.ANY)
    return pl.pallas_call(
        lambda *_: None,
        out_shape=jax.ShapeDtypeStruct(value.shape, value.dtype),
        in_specs=[anywhere, anywhere],
        out_specs=anywhere,
        input_output_aliases={0: 0},
        compiler_params=pltpu.CompilerParams(vmem_limit_bytes=VMEM_BYTES),
    )(value, first)


def fill_kernel(places, out_at, *refs):
    out_ref, sems = refs[out_at], refs[-1]
    for tile_ref in refs[out_at + 1 : -1]:
        tile_ref[...] = jnp.zeros_like(tile_ref)
    at = lax.axis_index("fsdp")
    chip, core = at // 2, at % 2
    copies = []
    for j, (step, swapped, row) in enumerate(places):
        sender = (chip + SIDE - step + 2 * step * core) % SIDE
        column = pl.multiple_of((sender * 2 + (1 - core if swapped else core)) * WIDTH, WIDTH)
        height = refs[j].shape[0] // CUTS
        for cut in range(CUTS):
            source = refs[j].at[pl.ds(cut * height, height), :]
            target = out_ref.at[pl.ds(row + cut * height, height), pl.ds(column, WIDTH)]
            copies.append(pltpu.make_async_copy(source, target, sems.at[len(copies)]))
    for copy in copies:
        copy.start()
    for copy in copies:
        copy.wait()


def fill(places, blocks, weights=None, tile=False):
    anywhere = pl.BlockSpec(memory_space=pl.ANY)
    given = [] if weights is None else [weights]
    return pl.pallas_call(
        functools.partial(fill_kernel, places, len(blocks) + len(given)),
        out_shape=[pltpu.HBM((BLOCK, D), jnp.bfloat16)] + [jax.ShapeDtypeStruct((8, 128), jnp.float32)] * tile,
        in_specs=[anywhere] * len(blocks) + [anywhere] * len(given),
        out_specs=[anywhere] + [pl.BlockSpec((8, 128), lambda: (0, 0))] * tile,
        scratch_shapes=[pltpu.SemaphoreType.DMA((CUTS * len(blocks),))],
        input_output_aliases={len(blocks): 0} if given else {},
        compiler_params=pltpu.CompilerParams(vmem_limit_bytes=VMEM_BYTES),
        cost_estimate=pl.CostEstimate(flops=0, bytes_accessed=0, transcendentals=0),
    )(*map(in_vmem, blocks), *given)


def along_y(value):
    pairs = [(y * 2 + core, (y + 1 - 2 * core) % SIDE * 2 + core) for y in range(SIDE) for core in range(2)]
    return lax.ppermute(value, "fsdp", pairs)


def to_other_core(value):
    return lax.ppermute(value, "fsdp", [(i, i ^ 1) for i in range(8)])


def gather(low, state):
    one = along_y(low)
    other = to_other_core(low)
    one_other = along_y(other)
    one = after(one, state)
    two = along_y(one)
    one_swapped = to_other_core(one)
    halves = [to_other_core(one_other[row : row + PART]) for row in (0, PART)]
    near = ((0, False, 0), (0, True, 0), (1, False, 0), (1, True, 0), (-1, True, 0), (-1, False, 0), (-1, False, PART))
    weights, filled = fill(near, (low, other, one, one_other, one_swapped, *halves), tile=True)
    two = after(two, filled)
    two_swapped = to_other_core(two)
    weights = fill(((2, False, 0),), (two,), weights)[0]
    return fill(((2, True, 0),), (two_swapped,), weights)[0]


def on_device(grad_shards, hadamard_signs, scale_index, scale_table, master, mean_moment, var_moment):
    grad, scale_index, master, mean_moment, var_moment = map(in_hbm, (grad_shards[0], scale_index, master, mean_moment, var_moment))
    scale_table = in_hbm(scale_table)
    place = (lax.axis_index("dp") * 2 + (lax.axis_index("fsdp") & 1)).reshape(1)
    sign = in_hbm(hadamard_signs)
    hmat = in_hbm(jnp.asarray(hadamard(TILE)))
    *state, staged = stage(master, mean_moment, var_moment)
    terms = reduce_scatter(place, scale_table, sign, grad, scale_index, hmat, staged)
    plain, square = decode(place, scale_table, sign, terms, scale_index, hmat, lax.axis_size(("dp", "fsdp")))
    square = lax.all_to_all(square, ("dp", "fsdp"), 0, 0, tiled=True)
    state = [in_vmem(v) for v in (plain, *state)]
    low = adamw(weights_kernel, jax.ShapeDtypeStruct((BLOCK, WIDTH), jnp.bfloat16), square, *state)
    new_state = adamw(state_kernel, (jax.ShapeDtypeStruct(master.shape, jnp.float32),) * 3, square, *state)
    return *new_state, gather(low, in_hbm(new_state[0]))


def solution(mesh):
    return jax.shard_map(
        on_device,
        mesh=mesh,
        in_specs=(
            P("dp", None, "fsdp"),
            P("fsdp"),
            P("fsdp", None),
            P(),
            P("dp", "fsdp"),
            P("dp", "fsdp"),
            P("dp", "fsdp"),
        ),
        out_specs=(P("dp", "fsdp"), P("dp", "fsdp"), P("dp", "fsdp"), P("dp", None)),
        check_vma=False,
    )
```
